512 devices in a mesh: aa: 32 (over z, x_hi), ba: 16 (over x_lo, y, core).
Axes of the slice: x: 4 (x_hi: 2, x_lo: 2; x = x_hi * 2 + x_lo), y: 4, z: 16, core: 2. Of those that a mesh axis runs over, the one named last changes fastest.
Arguments:
- features_a: bfloat16 [64, 32, 256], P('aa', 'ba'), may hold values from -9 to 9
- features_b: bfloat16 [64, 128, 256], P('ba', 'aa'), may hold values from -9 to 9
- conv_in: float32 [8, 3, 3, 3, 3], replicated, may hold values from -0.625 to 0.625
- bias_in: float32 [8], replicated, may hold values from -1 to 1
- conv_out: float32 [8, 3, 3, 3, 3], replicated, may hold values from -0.25 to 0.25
Outputs:
- log_mutual: float32 [64, 32, 64, 128], P('aa', None, 'ba')
- warped: float32 [64, 32, 256], P('aa', 'ba')
The draws below stay inside these ranges and needn't reach their ends.
All inputs are finite; a program needn't handle non-finite values.
Results may differ from the reference program's by a relative error of at most 0.0035.
Values may be sent and summed in bfloat16 or wider, within the bound.
A program may use at most 64 MiB of HBM per device.

```python
import math
import jax
import jax.numpy as jnp
from jax import lax

C = 256
HID = 8
WA = 32
WB = 128
HA = 64
HB = 64


def draw_features_a(key, part):
    noise_key, scale_key = jax.random.split(jax.random.fold_in(key, 11))
    raw_noise = jax.random.truncated_normal(noise_key, -3.3, 3.3, (HA, WA, C))
    spread = jnp.exp(jax.random.uniform(scale_key, (HA, WA, 1), minval=math.log(0.4), maxval=math.log(2.0)))
    return (raw_noise * spread).astype(jnp.bfloat16)


def draw_features_b(key, part):
    noise_key, scale_key = jax.random.split(jax.random.fold_in(key, 13))
    raw_noise = jax.random.truncated_normal(noise_key, -3.3, 3.3, (HB, WB, C))
    spread = jnp.exp(jax.random.uniform(scale_key, (HB, WB, 1), minval=math.log(0.4), maxval=math.log(2.0)))
    return (raw_noise * spread).astype(jnp.bfloat16)


def scatter_about(key, shape, deviation, reach, held_as=jnp.bfloat16):
    values = deviation * jax.random.normal(key, shape, jnp.float32)
    return jnp.clip(values, min=-reach, max=reach).astype(held_as)


def setup_inputs(seed: int = 0) -> dict:
    seeds = jax.random.split(jax.random.key(seed), 6)
    features_a = draw_features_a(jax.random.fold_in(seeds[5], 71), 0)
    features_b = draw_features_b(jax.random.fold_in(seeds[5], 71), 0)
    conv_in = scatter_about(seeds[2], (HID, 3, 3, 3, 3), 81 ** -0.5, 0.625, jnp.float32)
    bias_in = jnp.clip(jax.random.uniform(seeds[3], (HID,), jnp.float32, -1.0, 1.0), -1.0, 1.0)
    conv_out = scatter_about(seeds[4], (HID, 3, 3, 3, 3), (HID * 81) ** -0.5, 0.25, jnp.float32)
    return dict(features_a=features_a, features_b=features_b, conv_in=conv_in, bias_in=bias_in, conv_out=conv_out)


def tap_offsets():
    return [(step_one, step_two, step_three, step_four) for step_one in range(3) for step_two in range(3) for step_three in range(3) for step_four in range(3)]

def window_sum(padded, kernel):
    extent = [size_here - 2 for size_here in padded.shape]
    result = jnp.zeros(extent, jnp.float32)
    for offsets in tap_offsets():
        window = padded[offsets[0]:offsets[0] + extent[0], offsets[1]:offsets[1] + extent[1], offsets[2]:offsets[2] + extent[2], offsets[3]:offsets[3] + extent[3]]
        result = result + kernel[offsets] * window
    return result

def dual_logsumexp(values):
    top_over_a = lax.optimization_barrier(jnp.max(values, axis=(0, 1), keepdims=True))
    norm_over_a = top_over_a + jnp.log(lax.optimization_barrier(jnp.sum(jnp.exp(values - top_over_a), axis=(0, 1), keepdims=True)))
    top_over_b = lax.optimization_barrier(jnp.max(values, axis=(2, 3), keepdims=True))
    norm_over_b = top_over_b + jnp.log(lax.optimization_barrier(jnp.sum(jnp.exp(values - top_over_b), axis=(2, 3), keepdims=True)))
    return (norm_over_a, norm_over_b)

def reference(features_a, features_b, conv_in, bias_in, conv_out):
    flat_a = features_a.reshape(HA * WA, C)
    flat_b = features_b.reshape(HB * WB, C)
    scores = (jnp.dot(flat_a, flat_b.T, preferred_element_type=jnp.float32) / math.sqrt(C)).reshape(HA, WA, HB, WB)
    offset = math.log(HA * WA * HB * WB)
    norm_a, norm_b = dual_logsumexp(scores)
    matched = jax.nn.softplus(2.0 * scores - norm_a - norm_b + offset)
    padded = jnp.pad(matched, 1)
    filtered = jnp.zeros(scores.shape, jnp.float32)
    for channel in range(HID):
        hidden = jax.nn.relu(window_sum(padded, conv_in[channel]) + bias_in[channel])
        filtered = filtered + window_sum(jnp.pad(hidden, 1), conv_out[channel])
    refined = scores + jax.nn.relu(filtered)
    norm_a2, norm_b2 = dual_logsumexp(refined)
    log_mutual = 2.0 * refined - norm_a2 - norm_b2 + offset
    weights = jnp.exp(refined - norm_b2).astype(jnp.bfloat16).reshape(HA * WA, HB * WB)
    warped = jnp.dot(weights, flat_b, preferred_element_type=jnp.float32).reshape(HA, WA, C)
    return (log_mutual, warped)
```

```python
import math

import jax
import jax.numpy as jnp
from jax import lax
from jax.experimental import pallas as pl
from jax.experimental.pallas import tpu as pltpu
from jax.sharding import PartitionSpec as P

F32, BF16, I32 = jnp.float32, jnp.bfloat16, jnp.int32
MESH = pl.DeviceIdType.MESH
OFFSET = math.log(64 * 32 * 64 * 128)
FAR = 1e30

AA_STEPS = sorted(
    [(dz, dx) for dz in range(-7, 9) for dx in range(2) if dz or dx],
    key=lambda o: -(abs(o[0]) + 2 * o[1]),
)
BA_STEPS = [15, 14, 13, 12, 11, 10, 9, 8, 7, 6, 5, 4, 3, 2, 1]
NEAR = [1, -1, 2, -2, 3, -3, 4, -4]


def iota(shape, dim):
    return lax.broadcasted_iota(I32, shape, dim)


def div(x, by):
    return (x * {3: 21846, 9: 7282, 27: 2428, 48: 1366}[by]) >> 16


def one_hot(mask):
    return jnp.where(mask, 1.0, 0.0).astype(BF16)


def dot(a, b):
    return jnp.dot(a, b, preferred_element_type=F32)


def dot_nt(a, b):
    return lax.dot_general(a, b, (((1,), (1,)), ((), ())), preferred_element_type=F32)


def halves(x):
    high = x.astype(BF16)
    return high, (x - high.astype(F32)).astype(BF16)


def select(chosen, x):
    high, low = halves(x)
    return dot(chosen, high) + dot(chosen, low)


def to_row(column):
    wide = jnp.broadcast_to(column, (64, 128))
    return jnp.concatenate([wide, wide], axis=0).T[0:1, 0:64]


def to_column(row):
    return jnp.broadcast_to(row, (128, 128)).T[0:64, 0:1]


def masses(cells):
    top_c = jnp.max(cells, axis=0, keepdims=True)
    lse_c = top_c + jnp.log(jnp.sum(jnp.exp(cells - top_c), axis=0, keepdims=True))
    top_r = jnp.max(cells, axis=1, keepdims=True)
    share = jnp.exp(cells - top_r)
    sum_r = jnp.sum(share, axis=1, keepdims=True)
    return lse_c, top_r, sum_r, share


def join(parts):
    top = jnp.max(parts, axis=0)
    return top + jnp.log(jnp.sum(jnp.exp(parts - top[None]), axis=0))


def kernel(
    pa, pb, wts, lm, warped,
    ga, gb, ax, bx, perm_b, w1f, w1, w2f, w2,
    na_src, nb_src, na_all, nb_all, na_own, nb_own, na_lo, na_hi, nb_lo, nb_hi,
    own, sx, xt, x3, x3_low, zs, ft, rn, pn, ps, pr,
    na2_src, nb2_src, na2_all, nb2_all, nar,
    s_a, r_a, s_b, r_b, s_h, r_h, s_na, r_na, s_nb, r_nb, s_na2, r_na2, s_nb2, r_nb2, s_p, r_p,
):
    me_a, me_b = lax.axis_index("aa"), lax.axis_index("ba")
    z, xh = me_a >> 1, me_a & 1

    def at(dz, dx=0):
        return ((((z + dz) & 15) << 1) | ((xh + dx) & 1), me_b)

    def send(src, dst, s, r, to):
        copy = pltpu.make_async_remote_copy(
            src_ref=src, dst_ref=dst, send_sem=s, recv_sem=r, device_id=to, device_id_type=MESH
        )
        copy.start()
        pending.append(copy)

    def arrived(ref, r):
        pltpu.make_async_remote_copy(
            src_ref=ref, dst_ref=ref, send_sem=r, recv_sem=r, device_id=at(0, 1), device_id_type=MESH
        ).wait_recv()

    pending = []

    barrier = pltpu.get_barrier_semaphore()
    greet = [at(d) for d in NEAR] + [at(0, 1), at(4, 1), at(-4, 1)]
    greet += [(me_a, (me_b + d) & 15) for d in BA_STEPS]
    for peer in greet:
        pl.semaphore_signal(barrier, inc=1, device_id=peer, device_id_type=MESH)

    ga[pl.ds(me_b, 1)] = pa[...][None]
    gb[pl.ds(me_a, 1)] = pb[...][None]
    row = iota((512, 128), 0)
    src = ((row >> 2) & 31) * 16 + (row >> 7) * 4 + (row & 3)
    for g in range(4):
        perm_b[:, g * 128 : (g + 1) * 128] = one_hot(src == iota((512, 128), 1) + g * 128)
    row = iota((64, 256), 0)
    perm_a = one_hot(((row & 31) >> 1) * 16 + (row >> 5) * 2 + (row & 1) == iota((64, 256), 1))

    pl.semaphore_wait(barrier, len(greet))

    for k, d in enumerate(NEAR):
        send(pb, gb.at[me_a], s_b.at[k], r_b.at[me_a], at(d))
    send(pb, gb.at[me_a], s_b.at[8], r_b.at[me_a], at(0, 1))
    for k, d in enumerate(BA_STEPS):
        send(pa, ga.at[me_b], s_a.at[k], r_a.at[me_b], (me_a, (me_b + d) & 15))

    col = iota((8, 512), 1)
    d24 = div(col, 48)
    rest = col - 48 * d24
    a1, b1 = rest >> 3, rest & 7
    d2 = (d24 * 11) >> 5
    tap = a1 * 27 + d2 * 9 + b1 * 3 + (d24 - 3 * d2)
    tap = jnp.where((a1 < 3) & (b1 < 3) & (col < 432), tap, -1)
    spread = one_hot(iota((128, 512), 0) == jnp.broadcast_to(tap[0:1], (128, 512)))
    high, low = halves(wts[:, 0:128])
    base = dot(high, spread) + dot(low, spread)
    for p in range(24):
        s = (p // 6) * 8 + p % 6
        w1f[p * 8 : p * 8 + 8] = pltpu.roll(base, s, 1) if s else base
    w1[0:192], w1[192:384] = halves(w1f[:, 0:432])

    k, c = iota((128, 256), 0), iota((128, 256), 1)
    k3, k9, k27 = div(k, 3), div(k, 9), div(k, 27)
    ca = div(c, 48)
    cb = (c - 48 * ca) >> 3
    pick = one_hot(iota((8, 256), 0) == (iota((8, 256), 1) & 7))
    taps = sum(
        lax.dot_general(part, pick, (((0,), (0,)), ((), ())), preferred_element_type=F32)
        for part in halves(wts[:, 128:256])
    )
    taps = jnp.where((k27 == ca) & (k3 - 3 * k9 == cb), taps, 0.0)
    k = iota((16, 128), 1)
    k3, k9, k27 = div(k, 3), div(k, 9), div(k, 27)
    place = one_hot(iota((16, 128), 0) == (k9 - 3 * k27) * 3 + (k - 3 * k3))
    base = select(place, taps)
    for o in range(8):
        s = (o // 4) * 48 + (o % 4) * 8
        w2f[o * 16 : o * 16 + 16] = pltpu.roll(base, s, 1) if s else base
    r, c = iota((72, 128), 0), iota((72, 128), 1)
    order = one_hot(c == (r & 7) * 16 + (r >> 3))
    c = iota((72, 256), 1)
    ca = div(c, 48)
    cb = (c - 48 * ca) >> 3
    ra, rb = 2 * me_a - 1 + ca, 4 * me_b - 1 + cb
    inside = (ra >= 0) & (ra < 64) & (rb >= 0) & (rb < 64)
    w2[0:72], w2[72:144] = halves(jnp.where(inside, select(order, w2f[...]), 0.0))
    bias = wts[:, 256:384]
    bias = jnp.concatenate([jnp.concatenate([bias] * 24, axis=0)] * 4, axis=1)
    for x in (x3, x3_low):
        x[:, 0:128] = jnp.zeros((144, 128), BF16)
        x[:, 33 * 128 :] = jnp.zeros((144, 128), BF16)
    zs[:, 0:128] = jnp.zeros((72, 128), F32)
    zs[:, 33 * 128 :] = jnp.zeros((72, 128), F32)
    nb_src[...] = jnp.zeros((1, 128), F32)
    nb2_src[...] = jnp.zeros((1, 128), F32)
    ps[...] = jnp.zeros((256, 128), F32)

    n = 9
    for d in NEAR:
        slot = at(d)[0]
        arrived(gb.at[slot], r_b.at[slot])
        targets = [at(0, 1)]
        if d != 4:
            targets = [at(-4 if d > 0 else 4, 1), at(-4 if d > 0 else 4), at(0, 1)]
        for to in targets:
            send(gb.at[slot], gb.at[slot], s_b.at[n], r_b.at[slot], to)
            n += 1
    for d in BA_STEPS:
        slot = (me_b + d) & 15
        arrived(ga.at[slot], r_a.at[slot])
    ax[64:128] = dot(perm_a, ga[...].reshape(256, 256)).astype(BF16)
    for d, dx in reversed(AA_STEPS):
        if dx or abs(d) > 4:
            slot = at(d, dx)[0]
            arrived(gb.at[slot], r_b.at[slot])
    bx[256:768] = dot(perm_b[...], gb[...].reshape(512, 256)).astype(BF16)

    up_a, down_a = ((me_a + 1) & 31, me_b), ((me_a - 1) & 31, me_b)
    up_b, down_b = (me_a, (me_b + 1) & 15), (me_a, (me_b - 1) & 15)
    send(bx.at[512:768], bx.at[0:256], s_h.at[0], r_h.at[0], up_b)
    send(bx.at[256:512], bx.at[768:1024], s_h.at[1], r_h.at[1], down_b)
    send(ax.at[64:128], ax.at[0:64], s_h.at[2], r_h.at[2], up_a)
    send(ax.at[64:128], ax.at[128:192], s_h.at[3], r_h.at[3], down_a)

    scores = dot_nt(ax[64:128], bx[256:768]) * (1.0 / 16.0)
    own[...] = scores
    lse_c, top_r, sum_r, _ = masses(scores)
    for b in range(4):
        na_src[b : b + 1] = lse_c[:, b * 128 : (b + 1) * 128]
    nb_src[:, 0:64] = to_row(top_r + jnp.log(sum_r))
    for k, (dz, dx) in enumerate(AA_STEPS):
        send(na_src, na_all.at[me_a], s_na.at[k], r_na.at[me_a], at(dz, dx))
    for k, d in enumerate(BA_STEPS):
        send(nb_src, nb_all.at[me_b], s_nb.at[k], r_nb.at[me_b], (me_a, (me_b + d) & 15))
    na_all[pl.ds(me_a, 1)] = na_src[...][None]
    nb_all[pl.ds(me_b, 1)] = nb_src[...][None]

    arrived(bx.at[0:256], r_h.at[0])
    arrived(bx.at[768:1024], r_h.at[1])
    arrived(ax.at[0:64], r_h.at[2])
    arrived(ax.at[128:192], r_h.at[3])
    for t in range(3):
        sx[t * 64 : t * 64 + 64] = dot_nt(ax[t * 64 : t * 64 + 64], bx[...]) * (1.0 / 8.0)

    for d in BA_STEPS:
        slot = (me_b + d) & 15
        arrived(nb_all.at[slot], r_nb.at[slot])
    nb_own[...] = join(nb_all[...])
    send(nb_own, nb_lo, s_h.at[4], r_h.at[4], up_a)
    send(nb_own, nb_hi, s_h.at[5], r_h.at[5], down_a)
    for dz, dx in reversed(AA_STEPS):
        slot = at(dz, dx)[0]
        arrived(na_all.at[slot], r_na.at[slot])
    na_own[...] = join(na_all[...])
    send(na_own, na_lo, s_h.at[6], r_h.at[6], up_b)
    send(na_own, na_hi, s_h.at[7], r_h.at[7], down_b)
    arrived(nb_lo, r_h.at[4])
    arrived(nb_hi, r_h.at[5])
    cols = [
        to_column(jnp.where(me_a > 0, nb_lo[...], FAR)),
        to_column(nb_own[...]),
        to_column(jnp.where(me_a < 31, nb_hi[...], FAR)),
    ]
    arrived(na_lo, r_h.at[6])
    arrived(na_hi, r_h.at[7])
    nar[0:2] = jnp.where(me_b > 0, na_lo[2:4], FAR) - OFFSET
    nar[2:6] = na_own[...] - OFFSET
    nar[6:8] = jnp.where(me_b < 15, na_hi[0:2], FAR) - OFFSET

    for t in range(3):
        for b in range(8):
            v = sx[t * 64 : t * 64 + 64, b * 128 : (b + 1) * 128] - cols[t] - nar[b : b + 1]
            v = jnp.maximum(v, 0.0) + jnp.log(1.0 + jnp.exp(-jnp.abs(v)))
            xt[pl.ds(t * 512 + b, 64, stride=8), :] = v
    lane = iota((48, 128), 1)
    for a2 in range(32):
        rows = [xt[pl.ds(((t * 2 + a) * 32 + a2) * 8, 8), :] for t in range(3) for a in range(2)]
        m = jnp.concatenate(rows, axis=0)
        out = slice((a2 + 1) * 128, (a2 + 2) * 128)
        x3[0:48, out], x3_low[0:48, out] = halves(jnp.where(lane > 0, pltpu.roll(m, 1, 1), 0.0))
        x3[48:96, out], x3_low[48:96, out] = halves(m)
        x3[96:144, out], x3_low[96:144, out] = halves(jnp.where(lane < 127, pltpu.roll(m, 127, 1), 0.0))
    for g in range(8):
        at2 = g * 512
        high, low = (
            jnp.concatenate([x[:, at2 + d * 128 : at2 + d * 128 + 512] for d in range(3)], axis=0)
            for x in (x3, x3_low)
        )
        hidden = dot(w1[...], high)
        hidden = hidden[0:192] + hidden[192:384] + dot(w1[0:192], low)
        high, low = halves(jnp.maximum(hidden + bias, 0.0))
        out = dot(w2[:, 0:192], high)
        zs[:, at2 + 128 : at2 + 640] = out[0:72] + out[72:144] + dot(w2[0:72, 0:192], low)
    lane = iota((8, 128), 1)
    for a2 in range(32):
        u = []
        for d4 in range(3):
            terms = [
                zs[(d * 3 + d4) * 8 : (d * 3 + d4) * 8 + 8, (a2 + d) * 128 : (a2 + d + 1) * 128]
                for d in range(3)
            ]
            u.append(terms[0] + terms[1] + terms[2])
        f = u[1] + jnp.where(lane > 0, pltpu.roll(u[0], 1, 1), 0.0)
        f = f + jnp.where(lane < 127, pltpu.roll(u[2], 127, 1), 0.0)
        ft[a2 * 8 : a2 * 8 + 8] = jnp.maximum(f, 0.0)
    for a in range(2):
        for b in range(4):
            rows, lanes = slice(a * 32, a * 32 + 32), slice(b * 128, (b + 1) * 128)
            rn[rows, lanes] = own[rows, lanes] + ft[pl.ds(a * 4 + b, 32, stride=8), :]

    refined = rn[...]
    lse_c, top_r, sum_r, share = masses(refined)
    for b in range(4):
        na2_src[b : b + 1] = lse_c[:, b * 128 : (b + 1) * 128]
    for k, (dz, dx) in enumerate(AA_STEPS):
        send(na2_src, na2_all.at[me_a], s_na2.at[k], r_na2.at[me_a], at(dz, dx))
    lse_r = top_r + jnp.log(sum_r)
    nb2_src[:, 0:64] = to_row(lse_r)
    for k, d in enumerate(BA_STEPS):
        send(nb2_src, nb2_all.at[me_b], s_nb2.at[k], r_nb2.at[me_b], (me_a, (me_b + d) & 15))
    na2_all[pl.ds(me_a, 1)] = na2_src[...][None]
    nb2_all[pl.ds(me_b, 1)] = nb2_src[...][None]
    high, low = halves(share)
    features = bx[256:768]
    moved = (dot(high, features) + dot(low, features)) / sum_r
    pn[0:64] = moved[:, 0:128]
    pn[64:128] = moved[:, 128:256]
    pn[128:192] = jnp.broadcast_to(lse_r, (64, 128))
    for g in range(3):
        for q in range(4):
            rows = pl.ds(g * 64 + (q >> 1) * 32 + (q & 1), 16, stride=2)
            ps[pl.ds(g * 4 + q, 16, stride=16), :] = pn[rows, :]
    for k, d in enumerate(BA_STEPS):
        to = (me_b + d) & 15
        block = ps.at[pl.ds(pl.multiple_of(to * 16, 16), 16)]
        send(block, pr.at[me_b], s_p.at[k], r_p.at[me_b], (me_a, to))
    pr[pl.ds(me_b, 1)] = ps[pl.ds(pl.multiple_of(me_b * 16, 16), 16), :][None]

    for d in BA_STEPS:
        slot = (me_b + d) & 15
        arrived(nb2_all.at[slot], r_nb2.at[slot])
    col = to_column(join(nb2_all[...])) - OFFSET
    for d in BA_STEPS:
        slot = (me_b + d) & 15
        arrived(pr.at[slot], r_p.at[slot])
    lse = pr[:, 8:12, :]
    weight = jnp.exp(lse - jnp.max(lse, axis=0, keepdims=True))
    total = jnp.sum(weight, axis=0)
    warped[:, 0:128] = jnp.sum(weight * pr[:, 0:4, :], axis=0) / total
    warped[:, 128:256] = jnp.sum(weight * pr[:, 4:8, :], axis=0) / total
    twice = 2.0 * refined - col
    for dz, dx in reversed(AA_STEPS):
        slot = at(dz, dx)[0]
        arrived(na2_all.at[slot], r_na2.at[slot])
    norm = join(na2_all[...])
    for b in range(4):
        lm[pl.ds(b, 64, stride=4), :] = twice[:, b * 128 : (b + 1) * 128] - norm[b : b + 1]
    for copy in pending:
        copy.wait_send()


def local(features_a, features_b, conv_in, bias_in, conv_out):
    pa = jnp.pad(features_a.reshape(4, 256), ((0, 12), (0, 0)))
    pb = features_b.reshape(16, 256)
    wts = jnp.concatenate(
        [
            jnp.pad(conv_in.reshape(8, 81), ((0, 0), (0, 47))),
            jnp.pad(conv_out.reshape(8, 81), ((0, 0), (0, 47))),
            jnp.broadcast_to(bias_in[:, None], (8, 128)),
        ],
        axis=1,
    )
    dma = pltpu.SemaphoreType.DMA
    vmem = pltpu.VMEM
    lm, warped = pl.pallas_call(
        kernel,
        out_shape=(jax.ShapeDtypeStruct((256, 128), F32), jax.ShapeDtypeStruct((4, 256), F32)),
        in_specs=[pl.BlockSpec(memory_space=pltpu.VMEM)] * 3,
        out_specs=(pl.BlockSpec(memory_space=pltpu.VMEM),) * 2,
        scratch_shapes=[
            vmem((16, 16, 256), BF16), vmem((32, 16, 256), BF16),
            vmem((192, 256), BF16), vmem((1024, 256), BF16), vmem((512, 512), BF16),
            vmem((192, 512), F32), vmem((384, 432), BF16), vmem((128, 256), F32), vmem((144, 256), BF16),
            vmem((4, 128), F32), vmem((1, 128), F32), vmem((32, 4, 128), F32), vmem((16, 1, 128), F32),
            vmem((4, 128), F32), vmem((1, 128), F32), vmem((4, 128), F32), vmem((4, 128), F32),
            vmem((1, 128), F32), vmem((1, 128), F32),
            vmem((64, 512), F32), vmem((192, 1024), F32), vmem((1536, 128), F32),
            vmem((144, 34 * 128), BF16), vmem((144, 34 * 128), BF16), vmem((72, 34 * 128), F32), vmem((256, 128), F32),
            vmem((64, 512), F32), vmem((192, 128), F32), vmem((256, 128), F32), vmem((16, 16, 128), F32),
            vmem((4, 128), F32), vmem((1, 128), F32), vmem((32, 4, 128), F32), vmem((16, 1, 128), F32),
            vmem((8, 128), F32),
            dma((15,)), dma((16,)), dma((31,)), dma((32,)), dma((8,)), dma((8,)),
            dma((31,)), dma((32,)), dma((15,)), dma((16,)),
            dma((31,)), dma((32,)), dma((15,)), dma((16,)), dma((15,)), dma((16,)),
        ],
        compiler_params=pltpu.CompilerParams(
            collective_id=0, has_side_effects=True, vmem_limit_bytes=40 * 2**20
        ),
        cost_estimate=pl.CostEstimate(flops=2 * 10**9, bytes_accessed=10**6, transcendentals=10**6),
    )(pa, pb, wts)
    return lm.reshape(2, 32, 4, 128), warped.reshape(2, 2, 256)


def solution(mesh):
    placed = (P("aa", "ba", None), P("ba", "aa", None), P(), P(), P())
    return jax.shard_map(
        local,
        mesh=mesh,
        in_specs=placed,
        out_specs=(P("aa", None, "ba", None), P("aa", "ba", None)),
        check_vma=False,
    )
```

```python
import math

import jax
import jax.numpy as jnp
from jax import lax
from jax.experimental import pallas as pl
from jax.experimental.pallas import tpu as pltpu
from jax.sharding import PartitionSpec as P

F32, BF16, I32 = jnp.float32, jnp.bfloat16, jnp.int32
MESH = pl.DeviceIdType.MESH
OFFSET = math.log(64 * 32 * 64 * 128)
FAR = 1e30

AA_STEPS = sorted(
    [(dz, dx) for dz in range(-7, 9) for dx in range(2) if dz or dx],
    key=lambda o: -(abs(o[0]) + 2 * o[1]),
)
BA_STEPS = [15, 14, 13, 12, 11, 10, 9, 8, 7, 6, 5, 4, 3, 2, 1]
NEAR = [4, -4, 3, -3, 2, -2, 1, -1]


def iota(shape, dim):
    return lax.broadcasted_iota(I32, shape, dim)


def div(x, by):
    return (x * {3: 21846, 9: 7282, 27: 2428, 48: 1366}[by]) >> 16


def one_hot(mask):
    return jnp.where(mask, 1.0, 0.0).astype(BF16)


def dot(a, b):
    return jnp.dot(a, b, preferred_element_type=F32)


def dot_nt(a, b):
    return lax.dot_general(a, b, (((1,), (1,)), ((), ())), preferred_element_type=F32)


def halves(x):
    high = x.astype(BF16)
    return high, (x - high.astype(F32)).astype(BF16)


def select(chosen, x):
    high, low = halves(x)
    return dot(chosen, high) + dot(chosen, low)


def to_row(column):
    wide = jnp.broadcast_to(column, (64, 128))
    return jnp.concatenate([wide, wide], axis=0).T[0:1, 0:64]


def to_column(row):
    return jnp.broadcast_to(row, (128, 128)).T[0:64, 0:1]


def masses(cells):
    top_c = jnp.max(cells, axis=0, keepdims=True)
    lse_c = top_c + jnp.log(jnp.sum(jnp.exp(cells - top_c), axis=0, keepdims=True))
    top_r = jnp.max(cells, axis=1, keepdims=True)
    share = jnp.exp(cells - top_r)
    sum_r = jnp.sum(share, axis=1, keepdims=True)
    return lse_c, top_r, sum_r, share


def join(parts):
    top = jnp.max(parts, axis=0)
    return top + jnp.log(jnp.sum(jnp.exp(parts - top[None]), axis=0))


def kernel(
    fa_hbm, fb_hbm, ci_hbm, co_hbm, bias_hbm, lm, warped,
    fa, fb, ci, co, bias_row, stage, taps_m, pa, pb, ga, gb, ax, bx, perm_b, w1f, w1, w2f, w2,
    na_src, nb_src, na_all, nb_all, na_own, nb_own, na_lo, na_hi, nb_lo, nb_hi,
    own, sx, xt, x3, x3_low, zs, ft, rn, pn, ps, pr,
    na2_src, nb2_src, na2_all, nb2_all, nar,
    s_a, r_a, s_b, r_b, s_h, r_h, s_na, r_na, s_nb, r_nb, s_na2, r_na2, s_nb2, r_nb2, s_p, r_p, s_in,
):
    me_a, me_b = lax.axis_index("aa"), lax.axis_index("ba")
    z, xh = me_a >> 1, me_a & 1

    def at(dz, dx=0):
        return ((((z + dz) & 15) << 1) | ((xh + dx) & 1), me_b)

    def send(src, dst, s, r, to):
        copy = pltpu.make_async_remote_copy(
            src_ref=src, dst_ref=dst, send_sem=s, recv_sem=r, device_id=to, device_id_type=MESH
        )
        copy.start()

    def arrived(ref, r):
        pltpu.make_async_remote_copy(
            src_ref=ref, dst_ref=ref, send_sem=r, recv_sem=r, device_id=at(0, 1), device_id_type=MESH
        ).wait_recv()

    given = [
        pltpu.make_async_copy(src, dst, s_in.at[k])
        for k, (src, dst) in enumerate(
            [(fa_hbm, fa), (fb_hbm, fb), (ci_hbm, ci), (co_hbm, co), (bias_hbm, bias_row)]
        )
    ]
    for copy in given:
        copy.start()

    barrier = pltpu.get_barrier_semaphore()
    greet = [at(d, dx) for d in NEAR for dx in range(2)] + [at(0, 1)]
    greet += [(me_a, (me_b + d) & 15) for d in BA_STEPS]
    for peer in greet:
        pl.semaphore_signal(barrier, inc=1, device_id=peer, device_id_type=MESH)

    stage[0:16] = jnp.zeros((16, 256), F32)
    given[0].wait()
    for a in range(2):
        stage[a * 2 : a * 2 + 2] = fa[a].astype(F32)
    pa[...] = stage[0:16].astype(BF16)
    given[1].wait()
    for b in range(4):
        stage[16 + b * 4 : 20 + b * 4] = fb[b].astype(F32)
    pb[...] = stage[16:32].astype(BF16)
    ga[pl.ds(me_b, 1)] = pa[...][None]
    gb[pl.ds(me_a, 1)] = pb[...][None]
    pl.semaphore_wait(barrier, len(greet))
    for k, d in enumerate(NEAR):
        send(pb, gb.at[me_a], s_b.at[0], r_b.at[k], at(d))
    send(pb, gb.at[me_a], s_b.at[0], r_b.at[8], at(0, 1))
    for d in BA_STEPS:
        send(pa, ga.at[me_b], s_a.at[0], r_a.at[0], (me_a, (me_b + d) & 15))

    row = iota((512, 128), 0)
    src = ((row >> 2) & 31) * 16 + (row >> 7) * 4 + (row & 3)
    for g in range(4):
        perm_b[:, g * 128 : (g + 1) * 128] = one_hot(src == iota((512, 128), 1) + g * 128)
    row = iota((64, 256), 0)
    perm_a = one_hot(((row & 31) >> 1) * 16 + (row >> 5) * 2 + (row & 1) == iota((64, 256), 1))

    for d in reversed(NEAR):
        slot = at(d)[0]
        arrived(gb.at[slot], r_b.at[NEAR.index(-d)])
        targets = [at(0, 1)]
        if abs(d) == 4:
            away = [-4, -3, -2, -1] if d > 0 else [3, 2, 1]
            targets = [at(step, dx) for step in away for dx in (1, 0)] + targets
        for to in targets:
            send(gb.at[slot], gb.at[slot], s_b.at[0], r_b.at[8], to)
    arrived(ga.at[0:15], r_a.at[0])
    ax[64:128] = dot(perm_a, ga[...].reshape(256, 256)).astype(BF16)
    up_a, down_a = ((me_a + 1) & 31, me_b), ((me_a - 1) & 31, me_b)
    up_b, down_b = (me_a, (me_b + 1) & 15), (me_a, (me_b - 1) & 15)
    send(ax.at[64:128], ax.at[0:64], s_h.at[2], r_h.at[2], up_a)
    send(ax.at[64:128], ax.at[128:192], s_h.at[3], r_h.at[3], down_a)
    arrived(gb.at[0:23], r_b.at[8])
    bx[256:768] = dot(perm_b[...], gb[...].reshape(512, 256)).astype(BF16)

    send(bx.at[512:768], bx.at[0:256], s_h.at[0], r_h.at[0], up_b)
    send(bx.at[256:512], bx.at[768:1024], s_h.at[1], r_h.at[1], down_b)

    scores = dot_nt(ax[64:128], bx[256:768]) * (1.0 / 16.0)
    own[...] = scores
    lse_c, top_r, sum_r, _ = masses(scores)
    for b in range(4):
        na_src[b : b + 1] = lse_c[:, b * 128 : (b + 1) * 128]
    nb_src[...] = jnp.zeros((1, 128), F32)
    nb_src[:, 0:64] = to_row(top_r + jnp.log(sum_r))
    for dz, dx in AA_STEPS:
        send(na_src, na_all.at[me_a], s_na.at[0], r_na.at[0], at(dz, dx))
    for d in BA_STEPS:
        send(nb_src, nb_all.at[me_b], s_nb.at[0], r_nb.at[0], (me_a, (me_b + d) & 15))
    na_all[pl.ds(me_a, 1)] = na_src[...][None]
    nb_all[pl.ds(me_b, 1)] = nb_src[...][None]

    col = iota((8, 512), 1)
    d24 = div(col, 48)
    rest = col - 48 * d24
    a1, b1 = rest >> 3, rest & 7
    d2 = (d24 * 11) >> 5
    tap = (a1 * 9 + d2 * 3 + b1) * 8 + (d24 - 3 * d2)
    tap = jnp.where((a1 < 3) & (b1 < 3) & (col < 432), tap, -1)
    spread = one_hot(iota((256, 512), 0) == jnp.broadcast_to(tap[0:1], (256, 512)))
    taps_m[...] = jnp.zeros((512, 128), F32)
    for copy in given[2:]:
        copy.wait()
    for k in range(27):
        taps_m[k * 8 : k * 8 + 3, 0:8] = ci[k]
        taps_m[256 + k * 8 : 259 + k * 8, 0:8] = co[k]
    base = sum(
        lax.dot_general(part, spread, (((0,), (0,)), ((), ())), preferred_element_type=F32)
        for part in halves(taps_m[0:256])
    )[0:8]
    for p in range(24):
        s = (p // 6) * 8 + p % 6
        w1f[p * 8 : p * 8 + 8] = pltpu.roll(base, s, 1) if s else base
    w1[0:192], w1[192:384] = halves(w1f[:, 0:432])

    k, c = iota((256, 256), 0) >> 3, iota((256, 256), 1)
    k3 = (k * 11) >> 5
    k9 = div(k, 9)
    ca = div(c, 48)
    cb = (c - 48 * ca) >> 3
    pick = one_hot(iota((128, 256), 0) == (iota((128, 256), 1) & 7))
    high, low = halves(taps_m[256:512])
    taps = jnp.where((k9 == ca) & (k - 3 * k3 == cb), dot(high, pick) + dot(low, pick), 0.0)
    k = iota((16, 256), 1)
    k3, k9 = ((k >> 3) * 11) >> 5, div(k >> 3, 9)
    place = one_hot(iota((16, 256), 0) == (k3 - 3 * k9) * 3 + (k & 7))
    place = jnp.where((k & 7) < 3, place, jnp.zeros_like(place))
    base = select(place, taps)
    for o in range(8):
        s = (o // 4) * 48 + (o % 4) * 8
        w2f[o * 16 : o * 16 + 16] = pltpu.roll(base, s, 1) if s else base
    r, c = iota((72, 128), 0), iota((72, 128), 1)
    order = one_hot(c == (r & 7) * 16 + (r >> 3))
    c = iota((72, 256), 1)
    ca = div(c, 48)
    cb = (c - 48 * ca) >> 3
    ra, rb = 2 * me_a - 1 + ca, 4 * me_b - 1 + cb
    inside = (ra >= 0) & (ra < 64) & (rb >= 0) & (rb < 64)
    w2[0:72], w2[72:144] = halves(jnp.where(inside, select(order, w2f[...]), 0.0))
    bias = jnp.where(iota((8, 8), 0) == iota((8, 8), 1), bias_row[...], 0.0)
    bias = jnp.broadcast_to(jnp.sum(bias, axis=1, keepdims=True), (8, 128))
    bias = jnp.concatenate([jnp.concatenate([bias] * 24, axis=0)] * 4, axis=1)
    for x in (x3, x3_low):
        x[:, 0:128] = jnp.zeros((144, 128), BF16)
        x[:, 33 * 128 :] = jnp.zeros((144, 128), BF16)
    zs[:, 0:128] = jnp.zeros((72, 128), F32)
    zs[:, 33 * 128 :] = jnp.zeros((72, 128), F32)
    nb2_src[...] = jnp.zeros((1, 128), F32)
    ps[...] = jnp.zeros((256, 128), F32)

    arrived(bx.at[0:256], r_h.at[0])
    arrived(bx.at[768:1024], r_h.at[1])
    arrived(ax.at[0:64], r_h.at[2])
    arrived(ax.at[128:192], r_h.at[3])
    for t in range(3):
        sx[t * 64 : t * 64 + 64] = dot_nt(ax[t * 64 : t * 64 + 64], bx[...]) * (1.0 / 8.0)

    arrived(nb_all.at[0:15], r_nb.at[0])
    nb_own[...] = join(nb_all[...])
    send(nb_own, nb_lo, s_h.at[4], r_h.at[4], up_a)
    send(nb_own, nb_hi, s_h.at[5], r_h.at[5], down_a)
    arrived(na_all.at[0:31], r_na.at[0])
    na_own[...] = join(na_all[...])
    send(na_own, na_lo, s_h.at[6], r_h.at[6], up_b)
    send(na_own, na_hi, s_h.at[7], r_h.at[7], down_b)
    arrived(nb_lo, r_h.at[4])
    arrived(nb_hi, r_h.at[5])
    cols = [
        to_column(jnp.where(me_a > 0, nb_lo[...], FAR)),
        to_column(nb_own[...]),
        to_column(jnp.where(me_a < 31, nb_hi[...], FAR)),
    ]
    arrived(na_lo, r_h.at[6])
    arrived(na_hi, r_h.at[7])
    nar[0:2] = jnp.where(me_b > 0, na_lo[2:4], FAR) - OFFSET
    nar[2:6] = na_own[...] - OFFSET
    nar[6:8] = jnp.where(me_b < 15, na_hi[0:2], FAR) - OFFSET

    for t in range(3):
        for b in range(8):
            v = sx[t * 64 : t * 64 + 64, b * 128 : (b + 1) * 128] - cols[t] - nar[b : b + 1]
            v = jnp.maximum(v, 0.0) + jnp.log(1.0 + jnp.exp(-jnp.abs(v)))
            xt[pl.ds(t * 512 + b, 64, stride=8), :] = v
    lane = iota((48, 128), 1)
    for a2 in range(32):
        rows = [xt[pl.ds(((t * 2 + a) * 32 + a2) * 8, 8), :] for t in range(3) for a in range(2)]
        m = jnp.concatenate(rows, axis=0)
        out = slice((a2 + 1) * 128, (a2 + 2) * 128)
        x3[0:48, out], x3_low[0:48, out] = halves(jnp.where(lane > 0, pltpu.roll(m, 1, 1), 0.0))
        x3[48:96, out], x3_low[48:96, out] = halves(m)
        x3[96:144, out], x3_low[96:144, out] = halves(jnp.where(lane < 127, pltpu.roll(m, 127, 1), 0.0))
    for g in range(8):
        at2 = g * 512
        high, low = (
            jnp.concatenate([x[:, at2 + d * 128 : at2 + d * 128 + 512] for d in range(3)], axis=0)
            for x in (x3, x3_low)
        )
        hidden = dot(w1[...], high)
        hidden = hidden[0:192] + hidden[192:384] + dot(w1[0:192], low)
        high, low = halves(jnp.maximum(hidden + bias, 0.0))
        out = dot(w2[:, 0:192], high)
        zs[:, at2 + 128 : at2 + 640] = out[0:72] + out[72:144] + dot(w2[0:72, 0:192], low)
    lane = iota((8, 128), 1)
    for a2 in range(32):
        u = []
        for d4 in range(3):
            terms = [
                zs[(d * 3 + d4) * 8 : (d * 3 + d4) * 8 + 8, (a2 + d) * 128 : (a2 + d + 1) * 128]
                for d in range(3)
            ]
            u.append(terms[0] + terms[1] + terms[2])
        f = u[1] + jnp.where(lane > 0, pltpu.roll(u[0], 1, 1), 0.0)
        f = f + jnp.where(lane < 127, pltpu.roll(u[2], 127, 1), 0.0)
        ft[a2 * 8 : a2 * 8 + 8] = jnp.maximum(f, 0.0)
    for a in range(2):
        for b in range(4):
            rows, lanes = slice(a * 32, a * 32 + 32), slice(b * 128, (b + 1) * 128)
            rn[rows, lanes] = own[rows, lanes] + ft[pl.ds(a * 4 + b, 32, stride=8), :]

    refined = rn[...]
    lse_c, top_r, sum_r, share = masses(refined)
    for b in range(4):
        na2_src[b : b + 1] = lse_c[:, b * 128 : (b + 1) * 128]
    for dz, dx in AA_STEPS:
        send(na2_src, na2_all.at[me_a], s_na2.at[0], r_na2.at[0], at(dz, dx))
    lse_r = top_r + jnp.log(sum_r)
    nb2_src[:, 0:64] = to_row(lse_r)
    for d in BA_STEPS:
        send(nb2_src, nb2_all.at[me_b], s_nb2.at[0], r_nb2.at[0], (me_a, (me_b + d) & 15))
    na2_all[pl.ds(me_a, 1)] = na2_src[...][None]
    nb2_all[pl.ds(me_b, 1)] = nb2_src[...][None]
    high, low = halves(share)
    features = bx[256:768]
    moved = (dot(high, features) + dot(low, features)) / sum_r
    pn[0:64] = moved[:, 0:128]
    pn[64:128] = moved[:, 128:256]
    pn[128:192] = jnp.broadcast_to(lse_r, (64, 128))
    for g in range(3):
        for q in range(4):
            rows = pl.ds(g * 64 + (q >> 1) * 32 + (q & 1), 16, stride=2)
            ps[pl.ds(g * 4 + q, 16, stride=16), :] = pn[rows, :]
    for d in BA_STEPS:
        to = (me_b + d) & 15
        block = ps.at[pl.ds(pl.multiple_of(to * 16, 16), 16)]
        send(block, pr.at[me_b], s_p.at[0], r_p.at[0], (me_a, to))
    pr[pl.ds(me_b, 1)] = ps[pl.ds(pl.multiple_of(me_b * 16, 16), 16), :][None]

    arrived(nb2_all.at[0:15], r_nb2.at[0])
    col = to_column(join(nb2_all[...])) - OFFSET
    arrived(pr.at[0:15], r_p.at[0])
    lse = pr[:, 8:12, :]
    weight = jnp.exp(lse - jnp.max(lse, axis=0, keepdims=True))
    total = jnp.sum(weight, axis=0)
    for g in range(2):
        moved = jnp.sum(weight * pr[:, g * 4 : g * 4 + 4, :], axis=0) / total
        for a in range(2):
            warped[a, :, g * 128 : g * 128 + 128] = moved[a * 2 : a * 2 + 2]
    twice = 2.0 * refined - col
    arrived(na2_all.at[0:31], r_na2.at[0])
    norm = join(na2_all[...])
    for b in range(4):
        lm[pl.ds(b, 64, stride=4), :] = twice[:, b * 128 : (b + 1) * 128] - norm[b : b + 1]
    for ref, sem in [
        (gb.at[0:31], s_b.at[0]), (ga.at[0:15], s_a.at[0]), (na_all.at[0:31], s_na.at[0]), (nb_all.at[0:15], s_nb.at[0]),
        (na2_all.at[0:31], s_na2.at[0]), (nb2_all.at[0:15], s_nb2.at[0]), (pr.at[0:15], s_p.at[0]),
        (bx.at[0:256], s_h.at[0]), (bx.at[0:256], s_h.at[1]), (ax.at[0:64], s_h.at[2]), (ax.at[0:64], s_h.at[3]),
        (nb_own, s_h.at[4]), (nb_own, s_h.at[5]), (na_own, s_h.at[6]), (na_own, s_h.at[7]),
    ]:
        arrived(ref, sem)


def place_results(lm, warped, lm_out, warped_out, s):
    copies = [pltpu.make_async_copy(lm, lm_out, s.at[0]), pltpu.make_async_copy(warped, warped_out, s.at[1])]
    for copy in copies:
        copy.start()
    for copy in copies:
        copy.wait()


def local(features_a, features_b, conv_in, bias_in, conv_out):
    ci = conv_in.transpose(1, 2, 3, 4, 0).reshape(27, 3, 8)
    co = conv_out.transpose(1, 2, 3, 4, 0).reshape(27, 3, 8)
    dma = pltpu.SemaphoreType.DMA
    vmem = pltpu.VMEM
    lm, warped = pl.pallas_call(
        kernel,
        out_shape=(jax.ShapeDtypeStruct((256, 128), F32), jax.ShapeDtypeStruct((2, 2, 256), F32)),
        in_specs=[pl.BlockSpec(memory_space=pltpu.HBM)] * 5,
        out_specs=(pl.BlockSpec(memory_space=pltpu.VMEM),) * 2,
        scratch_shapes=[
            vmem((2, 2, 256), BF16), vmem((4, 4, 256), BF16), vmem((27, 3, 8), F32), vmem((27, 3, 8), F32), vmem((1, 8), F32),
            vmem((32, 256), F32), vmem((512, 128), F32), vmem((16, 256), BF16), vmem((16, 256), BF16),
            vmem((16, 16, 256), BF16), vmem((32, 16, 256), BF16),
            vmem((192, 256), BF16), vmem((1024, 256), BF16), vmem((512, 512), BF16),
            vmem((192, 512), F32), vmem((384, 432), BF16), vmem((128, 256), F32), vmem((144, 256), BF16),
            vmem((4, 128), F32), vmem((1, 128), F32), vmem((32, 4, 128), F32), vmem((16, 1, 128), F32),
            vmem((4, 128), F32), vmem((1, 128), F32), vmem((4, 128), F32), vmem((4, 128), F32),
            vmem((1, 128), F32), vmem((1, 128), F32),
            vmem((64, 512), F32), vmem((192, 1024), F32), vmem((1536, 128), F32),
            vmem((144, 34 * 128), BF16), vmem((144, 34 * 128), BF16), vmem((72, 34 * 128), F32), vmem((256, 128), F32),
            vmem((64, 512), F32), vmem((192, 128), F32), vmem((256, 128), F32), vmem((16, 16, 128), F32),
            vmem((4, 128), F32), vmem((1, 128), F32), vmem((32, 4, 128), F32), vmem((16, 1, 128), F32),
            vmem((8, 128), F32),
            dma((1,)), dma((1,)), dma((1,)), dma((9,)), dma((8,)), dma((8,)),
            dma((1,)), dma((1,)), dma((1,)), dma((1,)),
            dma((1,)), dma((1,)), dma((1,)), dma((1,)), dma((1,)), dma((1,)), dma((5,)),
        ],
        compiler_params=pltpu.CompilerParams(
            collective_id=0, has_side_effects=True, vmem_limit_bytes=60 * 2**20
        ),
        cost_estimate=pl.CostEstimate(flops=2 * 10**9, bytes_accessed=10**6, transcendentals=10**6),
    )(features_a, features_b, ci, co, bias_in.reshape(1, 8))
    lm = lm.reshape(2, 32, 4, 128)
    return pl.pallas_call(
        place_results,
        out_shape=(jax.ShapeDtypeStruct(lm.shape, F32), jax.ShapeDtypeStruct(warped.shape, F32)),
        in_specs=[pl.BlockSpec(memory_space=pltpu.VMEM)] * 2,
        out_specs=(pl.BlockSpec(memory_space=pltpu.HBM),) * 2,
        scratch_shapes=[dma((2,))],
        compiler_params=pltpu.CompilerParams(vmem_limit_bytes=60 * 2**20),
    )(lm, warped)


def solution(mesh):
    placed = (P("aa", "ba", None), P("ba", "aa", None), P(), P(), P())
    return jax.shard_map(
        local,
        mesh=mesh,
        in_specs=placed,
        out_specs=(P("aa", None, "ba", None), P("aa", "ba", None)),
        check_vma=False,
    )
```

```python
import math

import jax
import jax.numpy as jnp
from jax import lax
from jax.experimental import pallas as pl
from jax.experimental.pallas import tpu as pltpu
from jax.sharding import PartitionSpec as P

F32, BF16, I32 = jnp.float32, jnp.bfloat16, jnp.int32
MESH = pl.DeviceIdType.MESH
OFFSET = math.log(64 * 32 * 64 * 128)
FAR = 1e30

AA_STEPS = sorted(
    [(dz, dx) for dz in range(-7, 9) for dx in range(2) if dz or dx],
    key=lambda o: -(abs(o[0]) + 2 * o[1]),
)
BA_STEPS = [15, 14, 13, 12, 11, 10, 9, 8, 7, 6, 5, 4, 3, 2, 1]
NEAR = [4, -4, 3, -3, 2, -2, 1, -1]


def iota(shape, dim):
    return lax.broadcasted_iota(I32, shape, dim)


def div(x, by):
    return (x * {3: 21846, 9: 7282, 27: 2428, 48: 1366}[by]) >> 16


def one_hot(mask):
    return jnp.where(mask, 1.0, 0.0).astype(BF16)


def dot(a, b):
    return jnp.dot(a, b, preferred_element_type=F32)


def dot_nt(a, b):
    return lax.dot_general(a, b, (((1,), (1,)), ((), ())), preferred_element_type=F32)


def halves(x):
    high = x.astype(BF16)
    return high, (x - high.astype(F32)).astype(BF16)


def select(chosen, x):
    high, low = halves(x)
    return dot(chosen, high) + dot(chosen, low)


def to_row(column):
    wide = jnp.broadcast_to(column, (64, 128))
    return jnp.concatenate([wide, wide], axis=0).T[0:1, 0:64]


def to_column(row):
    return jnp.broadcast_to(row, (128, 128)).T[0:64, 0:1]


def masses(cells):
    top_c = jnp.max(cells, axis=0, keepdims=True)
    lse_c = top_c + jnp.log(jnp.sum(jnp.exp(cells - top_c), axis=0, keepdims=True))
    top_r = jnp.max(cells, axis=1, keepdims=True)
    share = jnp.exp(cells - top_r)
    sum_r = jnp.sum(share, axis=1, keepdims=True)
    return lse_c, top_r, sum_r, share


def join(parts):
    top = jnp.max(parts, axis=0)
    return top + jnp.log(jnp.sum(jnp.exp(parts - top[None]), axis=0))


def kernel(
    fa_hbm, fb_hbm, ci_hbm, co_hbm, bias_hbm, lm, warped,
    fa, fb, ci, co, bias_row, stage, taps_m, pa, pb, ga, gb, ax, bx, w1f, w1, w2f, w2,
    na_src, nb_src, na_all, nb_all, na_own, nb_own, na_lo, na_hi, nb_lo, nb_hi,
    own, sx, xt, x3, x3_low, acc, zs, ft, rn, pn, ps, pr,
    na2_src, nb2_src, na2_all, nb2_all, nar,
    s_a, r_a, s_b, r_b, s_h, r_h, s_na, r_na, s_nb, r_nb, s_na2, r_na2, s_nb2, r_nb2, s_p, r_p, s_in,
):
    me_a, me_b = lax.axis_index("aa"), lax.axis_index("ba")
    z, xh = me_a >> 1, me_a & 1

    def at(dz, dx=0):
        return ((((z + dz) & 15) << 1) | ((xh + dx) & 1), me_b)

    def send(src, dst, s, r, to):
        copy = pltpu.make_async_remote_copy(
            src_ref=src, dst_ref=dst, send_sem=s, recv_sem=r, device_id=to, device_id_type=MESH
        )
        copy.start()

    def arrived(ref, r):
        pltpu.make_async_remote_copy(
            src_ref=ref, dst_ref=ref, send_sem=r, recv_sem=r, device_id=at(0, 1), device_id_type=MESH
        ).wait_recv()

    given = [
        pltpu.make_async_copy(src, dst, s_in.at[k])
        for k, (src, dst) in enumerate(
            [(fa_hbm, fa), (fb_hbm, fb), (ci_hbm, ci), (co_hbm, co), (bias_hbm, bias_row)]
        )
    ]
    for copy in given:
        copy.start()

    barrier = pltpu.get_barrier_semaphore()
    greet = [at(d, dx) for d in NEAR for dx in range(2)] + [at(0, 1)]
    greet += [(me_a, (me_b + d) & 15) for d in BA_STEPS]
    for peer in greet:
        pl.semaphore_signal(barrier, inc=1, device_id=peer, device_id_type=MESH)

    stage[0:16] = jnp.zeros((16, 256), F32)
    given[0].wait()
    for a in range(2):
        stage[a * 2 : a * 2 + 2] = fa[a].astype(F32)
    pa[...] = stage[0:16].astype(BF16)
    given[1].wait()
    for b in range(4):
        stage[16 + b * 4 : 20 + b * 4] = fb[b].astype(F32)
    pb[...] = stage[16:32].astype(BF16)
    pl.semaphore_wait(barrier, len(greet))
    for k, d in enumerate(NEAR):
        send(pb, gb.at[me_a], s_b.at[0], r_b.at[k], at(d))
    send(pb, gb.at[me_a], s_b.at[0], r_b.at[8], at(0, 1))
    for d in BA_STEPS:
        send(pa, ga.at[me_b], s_a.at[0], r_a.at[0], (me_a, (me_b + d) & 15))

    ga[pl.ds(me_b, 1)] = pa[...][None]
    gb[pl.ds(me_a, 1)] = pb[...][None]

    row = iota((128, 128), 0)
    perm_b = one_hot(((row >> 2) & 7) * 16 + (row >> 5) * 4 + (row & 3) == iota((128, 128), 1))
    row = iota((64, 256), 0)
    perm_a = one_hot(((row & 31) >> 1) * 16 + (row >> 5) * 2 + (row & 1) == iota((64, 256), 1))

    for d in reversed(NEAR):
        slot = at(d)[0]
        arrived(gb.at[slot], r_b.at[NEAR.index(-d)])
        targets = [at(0, 1)]
        if abs(d) == 4:
            away = [-4, -3, -2, -1] if d > 0 else [3, 2, 1]
            targets = [at(step, dx) for step in away for dx in (1, 0)] + targets
        for to in targets:
            send(gb.at[slot], gb.at[slot], s_b.at[0], r_b.at[8], to)
    arrived(ga.at[0:15], r_a.at[0])
    ax[64:128] = dot(perm_a, ga[...].reshape(256, 256)).astype(BF16)
    up_a, down_a = ((me_a + 1) & 31, me_b), ((me_a - 1) & 31, me_b)
    up_b, down_b = (me_a, (me_b + 1) & 15), (me_a, (me_b - 1) & 15)
    send(ax.at[64:128], ax.at[0:64], s_h.at[2], r_h.at[2], up_a)
    send(ax.at[64:128], ax.at[128:192], s_h.at[3], r_h.at[3], down_a)
    arrived(gb.at[0:23], r_b.at[8])
    for g in range(4):
        rows = dot(perm_b, gb[g * 8 : g * 8 + 8].reshape(128, 256)).astype(BF16)
        for b in range(4):
            bx[256 + b * 128 + g * 32 : 288 + b * 128 + g * 32] = rows[b * 32 : b * 32 + 32]

    send(bx.at[512:768], bx.at[0:256], s_h.at[0], r_h.at[0], up_b)
    send(bx.at[256:512], bx.at[768:1024], s_h.at[1], r_h.at[1], down_b)

    scores = dot_nt(ax[64:128], bx[256:768]) * (1.0 / 16.0)
    own[...] = scores
    lse_c, top_r, sum_r, _ = masses(scores)
    for b in range(4):
        na_src[b : b + 1] = lse_c[:, b * 128 : (b + 1) * 128]
    nb_src[...] = jnp.zeros((1, 128), F32)
    nb_src[:, 0:64] = to_row(top_r + jnp.log(sum_r))
    for dz, dx in AA_STEPS:
        send(na_src, na_all.at[me_a], s_na.at[0], r_na.at[0], at(dz, dx))
    for d in BA_STEPS:
        send(nb_src, nb_all.at[me_b], s_nb.at[0], r_nb.at[0], (me_a, (me_b + d) & 15))
    na_all[pl.ds(me_a, 1)] = na_src[...][None]
    nb_all[pl.ds(me_b, 1)] = nb_src[...][None]

    col = iota((8, 512), 1)
    d24 = div(col, 48)
    rest = col - 48 * d24
    a1, b1 = rest >> 3, rest & 7
    d2 = (d24 * 11) >> 5
    tap = (a1 * 9 + d2 * 3 + b1) * 8 + (d24 - 3 * d2)
    tap = jnp.where((a1 < 3) & (b1 < 3) & (col < 432), tap, -1)
    spread = one_hot(iota((256, 512), 0) == jnp.broadcast_to(tap[0:1], (256, 512)))
    taps_m[...] = jnp.zeros((512, 128), F32)
    for copy in given[2:]:
        copy.wait()
    for k in range(27):
        taps_m[k * 8 : k * 8 + 3, 0:8] = ci[k]
        taps_m[256 + k * 8 : 259 + k * 8, 0:8] = co[k]
    base = sum(
        lax.dot_general(part, spread, (((0,), (0,)), ((), ())), preferred_element_type=F32)
        for part in halves(taps_m[0:256])
    )[0:8]
    for p in range(24):
        s = (p // 6) * 8 + p % 6
        w1f[p * 8 : p * 8 + 8] = pltpu.roll(base, s, 1) if s else base
    for g in range(4):
        c = iota((8, 128), 1) + (g & 1) * 128
        d2 = (c * 820) >> 16
        c = c - 80 * d2
        d4 = (c * 2731) >> 16
        c = jnp.where((d4 < 3) & (d2 < 3), c - 24 * d4, -1000)
        b1 = (c & 3) + (2 if g < 2 else ((c & 2) << 1))
        target = (d2 * 3 + d4) * 48 + (c >> 2) * 8 + b1
        chosen = one_hot(iota((512, 128), 0) == jnp.broadcast_to(target[0:1], (512, 128)))
        for part, rows in zip(halves(w1f[...]), (slice(0, 192), slice(192, 384))):
            w1[rows, g * 128 : g * 128 + 128] = dot(part, chosen).astype(BF16)

    k, c = iota((256, 256), 0) >> 3, iota((256, 256), 1)
    k3 = (k * 11) >> 5
    k9 = div(k, 9)
    ca = div(c, 48)
    cb = (c - 48 * ca) >> 3
    pick = one_hot(iota((128, 256), 0) == (iota((128, 256), 1) & 7))
    high, low = halves(taps_m[256:512])
    taps = jnp.where((k9 == ca) & (k - 3 * k3 == cb), dot(high, pick) + dot(low, pick), 0.0)
    k = iota((16, 256), 1)
    k3, k9 = ((k >> 3) * 11) >> 5, div(k >> 3, 9)
    place = one_hot(iota((16, 256), 0) == (k3 - 3 * k9) * 3 + (k & 7))
    place = jnp.where((k & 7) < 3, place, jnp.zeros_like(place))
    base = select(place, taps)
    for o in range(8):
        s = (o // 4) * 48 + (o % 4) * 8
        w2f[o * 16 : o * 16 + 16] = pltpu.roll(base, s, 1) if s else base
    r, c = iota((72, 128), 0), iota((72, 128), 1)
    order = one_hot(c == (r & 7) * 16 + (r >> 3))
    c = iota((72, 256), 1)
    ca = div(c, 48)
    cb = (c - 48 * ca) >> 3
    ra, rb = 2 * me_a - 1 + ca, 4 * me_b - 1 + cb
    inside = (ra >= 0) & (ra < 64) & (rb >= 0) & (rb < 64)
    w2[0:72], w2[72:144] = halves(jnp.where(inside, select(order, w2f[...]), 0.0))
    bias = jnp.where(iota((8, 8), 0) == iota((8, 8), 1), bias_row[...], 0.0)
    bias = jnp.broadcast_to(jnp.sum(bias, axis=1, keepdims=True), (8, 128))
    bias = jnp.concatenate([jnp.concatenate([bias] * 24, axis=0)] * 4, axis=1)
    for x in (x3, x3_low):
        x[:, 0:128] = jnp.zeros((160, 128), BF16)
        x[:, 33 * 128 :] = jnp.zeros((160, 128), BF16)
    zs[:, 0:128] = jnp.zeros((72, 128), F32)
    zs[:, 33 * 128 :] = jnp.zeros((72, 128), F32)
    nb2_src[...] = jnp.zeros((1, 128), F32)
    ps[...] = jnp.zeros((256, 128), F32)

    arrived(bx.at[0:256], r_h.at[0])
    arrived(bx.at[768:1024], r_h.at[1])
    arrived(ax.at[0:64], r_h.at[2])
    arrived(ax.at[128:192], r_h.at[3])
    for t in range(3):
        sx[t * 64 : t * 64 + 64] = dot_nt(ax[t * 64 : t * 64 + 64], bx[...]) * (1.0 / 8.0)

    arrived(nb_all.at[0:15], r_nb.at[0])
    nb_own[...] = join(nb_all[...])
    send(nb_own, nb_lo, s_h.at[4], r_h.at[4], up_a)
    send(nb_own, nb_hi, s_h.at[5], r_h.at[5], down_a)
    arrived(na_all.at[0:31], r_na.at[0])
    na_own[...] = join(na_all[...])
    send(na_own, na_lo, s_h.at[6], r_h.at[6], up_b)
    send(na_own, na_hi, s_h.at[7], r_h.at[7], down_b)
    arrived(nb_lo, r_h.at[4])
    arrived(nb_hi, r_h.at[5])
    cols = [
        to_column(jnp.where(me_a > 0, nb_lo[...], FAR)),
        to_column(nb_own[...]),
        to_column(jnp.where(me_a < 31, nb_hi[...], FAR)),
    ]
    nar[2:6] = na_own[...] - OFFSET
    lane = iota((24, 128), 1)

    def match(side, columns):
        for t in range(3):
            for k, b in enumerate(columns):
                v = sx[t * 64 : t * 64 + 64, b * 128 : (b + 1) * 128] - cols[t] - nar[b : b + 1]
                v = jnp.maximum(v, 0.0) + jnp.log(1.0 + jnp.exp(-jnp.abs(v)))
                for a in range(2):
                    xt[pl.ds(side * 768 + t * 256 + a * 4 + k, 32, stride=8), :] = v[a * 32 : a * 32 + 32]
        for a2 in range(32):
            m = jnp.concatenate([xt[pl.ds(side * 768 + (t * 32 + a2) * 8, 8), :] for t in range(3)], axis=0)
            left = jnp.where(lane > 0, pltpu.roll(m, 1, 1), 0.0)
            right = jnp.where(lane < 127, pltpu.roll(m, 127, 1), 0.0)
            m = jnp.concatenate([left, m, right, jnp.zeros((8, 128), F32)], axis=0)
            rows, out = slice(side * 80, side * 80 + 80), slice((a2 + 1) * 128, (a2 + 2) * 128)
            x3[rows, out], x3_low[rows, out] = halves(m)

    def first(side, at2):
        rows, taps = slice(side * 80, side * 80 + 80), slice(side * 256, side * 256 + 240)
        high, low = (
            jnp.concatenate([x[rows, at2 + d * 128 : at2 + d * 128 + 512] for d in range(3)], axis=0)
            for x in (x3, x3_low)
        )
        out = dot(w1[:, taps], high)
        return out[0:192] + out[192:384] + dot(w1[0:192, taps], low)

    match(0, (2, 3, 4, 5))
    for g in range(8):
        acc[:, g * 512 : g * 512 + 512] = first(0, g * 512) + bias
    arrived(na_lo, r_h.at[6])
    arrived(na_hi, r_h.at[7])
    nar[0:2] = jnp.where(me_b > 0, na_lo[2:4], FAR) - OFFSET
    nar[6:8] = jnp.where(me_b < 15, na_hi[0:2], FAR) - OFFSET
    match(1, (0, 1, 6, 7))
    for g in range(8):
        at2 = g * 512
        hidden = acc[:, at2 : at2 + 512] + first(1, at2)
        high, low = halves(jnp.maximum(hidden, 0.0))
        out = dot(w2[:, 0:192], high)
        zs[:, at2 + 128 : at2 + 640] = out[0:72] + out[72:144] + dot(w2[0:72, 0:192], low)
    lane = iota((8, 128), 1)
    for a2 in range(32):
        u = []
        for d4 in range(3):
            terms = [
                zs[(d * 3 + d4) * 8 : (d * 3 + d4) * 8 + 8, (a2 + d) * 128 : (a2 + d + 1) * 128]
                for d in range(3)
            ]
            u.append(terms[0] + terms[1] + terms[2])
        f = u[1] + jnp.where(lane > 0, pltpu.roll(u[0], 1, 1), 0.0)
        f = f + jnp.where(lane < 127, pltpu.roll(u[2], 127, 1), 0.0)
        ft[a2 * 8 : a2 * 8 + 8] = jnp.maximum(f, 0.0)
    for a in range(2):
        for b in range(4):
            rows, lanes = slice(a * 32, a * 32 + 32), slice(b * 128, (b + 1) * 128)
            rn[rows, lanes] = own[rows, lanes] + ft[pl.ds(a * 4 + b, 32, stride=8), :]

    refined = rn[...]
    lse_c, top_r, sum_r, share = masses(refined)
    for b in range(4):
        na2_src[b : b + 1] = lse_c[:, b * 128 : (b + 1) * 128]
    for dz, dx in AA_STEPS:
        send(na2_src, na2_all.at[me_a], s_na2.at[0], r_na2.at[0], at(dz, dx))
    lse_r = top_r + jnp.log(sum_r)
    nb2_src[:, 0:64] = to_row(lse_r)
    for d in BA_STEPS:
        send(nb2_src, nb2_all.at[me_b], s_nb2.at[0], r_nb2.at[0], (me_a, (me_b + d) & 15))
    na2_all[pl.ds(me_a, 1)] = na2_src[...][None]
    nb2_all[pl.ds(me_b, 1)] = nb2_src[...][None]
    high, low = halves(share)
    features = bx[256:768]
    moved = (dot(high, features) + dot(low, features)) / sum_r
    pn[0:64] = moved[:, 0:128]
    pn[64:128] = moved[:, 128:256]
    pn[128:192] = jnp.broadcast_to(lse_r, (64, 128))
    for g in range(3):
        for q in range(4):
            rows = pl.ds(g * 64 + (q >> 1) * 32 + (q & 1), 16, stride=2)
            ps[pl.ds(g * 4 + q, 16, stride=16), :] = pn[rows, :]
    for d in BA_STEPS:
        to = (me_b + d) & 15
        block = ps.at[pl.ds(pl.multiple_of(to * 16, 16), 16)]
        send(block, pr.at[me_b], s_p.at[0], r_p.at[0], (me_a, to))
    pr[pl.ds(me_b, 1)] = ps[pl.ds(pl.multiple_of(me_b * 16, 16), 16), :][None]

    arrived(nb2_all.at[0:15], r_nb2.at[0])
    col = to_column(join(nb2_all[...])) - OFFSET
    arrived(pr.at[0:15], r_p.at[0])
    lse = pr[:, 8:12, :]
    weight = jnp.exp(lse - jnp.max(lse, axis=0, keepdims=True))
    total = jnp.sum(weight, axis=0)
    for g in range(2):
        moved = jnp.sum(weight * pr[:, g * 4 : g * 4 + 4, :], axis=0) / total
        for a in range(2):
            warped[a, :, g * 128 : g * 128 + 128] = moved[a * 2 : a * 2 + 2]
    twice = 2.0 * refined - col
    arrived(na2_all.at[0:31], r_na2.at[0])
    norm = join(na2_all[...])
    for b in range(4):
        lm[pl.ds(b, 64, stride=4), :] = twice[:, b * 128 : (b + 1) * 128] - norm[b : b + 1]
    for ref, sem in [
        (gb.at[0:31], s_b.at[0]), (ga.at[0:15], s_a.at[0]), (na_all.at[0:31], s_na.at[0]), (nb_all.at[0:15], s_nb.at[0]),
        (na2_all.at[0:31], s_na2.at[0]), (nb2_all.at[0:15], s_nb2.at[0]), (pr.at[0:15], s_p.at[0]),
        (bx.at[0:256], s_h.at[0]), (bx.at[0:256], s_h.at[1]), (ax.at[0:64], s_h.at[2]), (ax.at[0:64], s_h.at[3]),
        (nb_own, s_h.at[4]), (nb_own, s_h.at[5]), (na_own, s_h.at[6]), (na_own, s_h.at[7]),
    ]:
        arrived(ref, sem)


def place_results(lm, warped, lm_out, warped_out, s):
    copies = [pltpu.make_async_copy(lm, lm_out, s.at[0]), pltpu.make_async_copy(warped, warped_out, s.at[1])]
    for copy in copies:
        copy.start()
    for copy in copies:
        copy.wait()


def local(features_a, features_b, conv_in, bias_in, conv_out):
    ci = conv_in.transpose(1, 2, 3, 4, 0).reshape(27, 3, 8)
    co = conv_out.transpose(1, 2, 3, 4, 0).reshape(27, 3, 8)
    dma = pltpu.SemaphoreType.DMA
    vmem = pltpu.VMEM
    lm, warped = pl.pallas_call(
        kernel,
        out_shape=(jax.ShapeDtypeStruct((256, 128), F32), jax.ShapeDtypeStruct((2, 2, 256), F32)),
        in_specs=[pl.BlockSpec(memory_space=pltpu.HBM)] * 5,
        out_specs=(pl.BlockSpec(memory_space=pltpu.VMEM),) * 2,
        scratch_shapes=[
            vmem((2, 2, 256), BF16), vmem((4, 4, 256), BF16), vmem((27, 3, 8), F32), vmem((27, 3, 8), F32), vmem((1, 8), F32),
            vmem((32, 256), F32), vmem((512, 128), F32), vmem((16, 256), BF16), vmem((16, 256), BF16),
            vmem((16, 16, 256), BF16), vmem((32, 16, 256), BF16),
            vmem((192, 256), BF16), vmem((1024, 256), BF16),
            vmem((192, 512), F32), vmem((384, 512), BF16), vmem((128, 256), F32), vmem((144, 256), BF16),
            vmem((4, 128), F32), vmem((1, 128), F32), vmem((32, 4, 128), F32), vmem((16, 1, 128), F32),
            vmem((4, 128), F32), vmem((1, 128), F32), vmem((4, 128), F32), vmem((4, 128), F32),
            vmem((1, 128), F32), vmem((1, 128), F32),
            vmem((64, 512), F32), vmem((192, 1024), F32), vmem((1536, 128), F32),
            vmem((160, 34 * 128), BF16), vmem((160, 34 * 128), BF16), vmem((192, 4096), F32), vmem((72, 34 * 128), F32), vmem((256, 128), F32),
            vmem((64, 512), F32), vmem((192, 128), F32), vmem((256, 128), F32), vmem((16, 16, 128), F32),
            vmem((4, 128), F32), vmem((1, 128), F32), vmem((32, 4, 128), F32), vmem((16, 1, 128), F32),
            vmem((8, 128), F32),
            dma((1,)), dma((1,)), dma((1,)), dma((9,)), dma((8,)), dma((8,)),
            dma((1,)), dma((1,)), dma((1,)), dma((1,)),
            dma((1,)), dma((1,)), dma((1,)), dma((1,)), dma((1,)), dma((1,)), dma((5,)),
        ],
        compiler_params=pltpu.CompilerParams(
            collective_id=0, has_side_effects=True, vmem_limit_bytes=60 * 2**20
        ),
        cost_estimate=pl.CostEstimate(flops=2 * 10**9, bytes_accessed=10**6, transcendentals=10**6),
    )(features_a, features_b, ci, co, bias_in.reshape(1, 8))
    lm = lm.reshape(2, 32, 4, 128)
    return pl.pallas_call(
        place_results,
        out_shape=(jax.ShapeDtypeStruct(lm.shape, F32), jax.ShapeDtypeStruct(warped.shape, F32)),
        in_specs=[pl.BlockSpec(memory_space=pltpu.VMEM)] * 2,
        out_specs=(pl.BlockSpec(memory_space=pltpu.HBM),) * 2,
        scratch_shapes=[dma((2,))],
        compiler_params=pltpu.CompilerParams(vmem_limit_bytes=60 * 2**20),
    )(lm, warped)


def solution(mesh):
    placed = (P("aa", "ba", None), P("ba", "aa", None), P(), P(), P())
    return jax.shard_map(
        local,
        mesh=mesh,
        in_specs=placed,
        out_specs=(P("aa", None, "ba", None), P("aa", "ba", None)),
        check_vma=False,
    )
```

```python
import math

import jax
import jax.numpy as jnp
from jax import lax
from jax.experimental import pallas as pl
from jax.experimental.pallas import tpu as pltpu
from jax.sharding import PartitionSpec as P

F32, BF16, I32 = jnp.float32, jnp.bfloat16, jnp.int32
MESH = pl.DeviceIdType.MESH
OFFSET = math.log(64 * 32 * 64 * 128)
FAR = 1e30
WIDE = 2048

AA_STEPS = sorted(
    [(dz, dx) for dz in range(-7, 9) for dx in range(2) if dz or dx],
    key=lambda o: -(abs(o[0]) + 2 * o[1]),
)
BA_STEPS = [15, 14, 13, 12, 11, 10, 9, 8, 7, 6, 5, 4, 3, 2, 1]
NEAR = [4, -4, 3, -3, 2, -2, 1, -1]


def iota(shape, dim):
    return lax.broadcasted_iota(I32, shape, dim)


def div(x, by):
    return (x * {3: 21846, 9: 7282, 27: 2428, 48: 1366}[by]) >> 16


def one_hot(mask):
    return jnp.where(mask, 1.0, 0.0).astype(BF16)


def dot(a, b):
    return jnp.dot(a, b, preferred_element_type=F32)


def dot_nt(a, b):
    return lax.dot_general(a, b, (((1,), (1,)), ((), ())), preferred_element_type=F32)


def halves(x):
    high = x.astype(BF16)
    return high, (x - high.astype(F32)).astype(BF16)


def select(chosen, x):
    high, low = halves(x)
    return dot(chosen, high) + dot(chosen, low)


def to_row(column):
    wide = jnp.broadcast_to(column, (64, 128))
    return jnp.concatenate([wide, wide], axis=0).T[0:1, 0:64]


def to_column(row):
    return jnp.broadcast_to(row, (128, 128)).T[0:64, 0:1]


def masses(cells):
    top_c = jnp.max(cells, axis=0, keepdims=True)
    lse_c = top_c + jnp.log(jnp.sum(jnp.exp(cells - top_c), axis=0, keepdims=True))
    top_r = jnp.max(cells, axis=1, keepdims=True)
    share = jnp.exp(cells - top_r)
    sum_r = jnp.sum(share, axis=1, keepdims=True)
    return lse_c, top_r, sum_r, share


def join(parts):
    top = jnp.max(parts, axis=0)
    return top + jnp.log(jnp.sum(jnp.exp(parts - top[None]), axis=0))


def kernel(
    fa_hbm, fb_hbm, ci_hbm, co_hbm, bias_hbm, lm, warped,
    fa, fb, ci, co, bias_row, stage, taps_m, pa, pb, ga, gb, ax, bx, w1f, w1, w2f, w2,
    na_src, nb_src, na_all, nb_all, na_own, nb_own, na_lo, na_hi, nb_lo, nb_hi,
    own, sx, xt, x3, x3_low, acc, zs, ft, rn, pn, ps, pr,
    na2_src, nb2_src, na2_all, nb2_all, nar,
    s_a, r_a, s_b, r_b, s_h, r_h, s_na, r_na, s_nb, r_nb, s_na2, r_na2, s_nb2, r_nb2, s_p, r_p, s_in,
):
    me_a, me_b = lax.axis_index("aa"), lax.axis_index("ba")
    z, xh = me_a >> 1, me_a & 1

    def at(dz, dx=0):
        return ((((z + dz) & 15) << 1) | ((xh + dx) & 1), me_b)

    def send(src, dst, s, r, to):
        copy = pltpu.make_async_remote_copy(
            src_ref=src, dst_ref=dst, send_sem=s, recv_sem=r, device_id=to, device_id_type=MESH
        )
        copy.start()

    def arrived(ref, r):
        pltpu.make_async_remote_copy(
            src_ref=ref, dst_ref=ref, send_sem=r, recv_sem=r, device_id=at(0, 1), device_id_type=MESH
        ).wait_recv()

    given = [
        pltpu.make_async_copy(src, dst, s_in.at[k])
        for k, (src, dst) in enumerate(
            [(fa_hbm, fa), (fb_hbm, fb), (ci_hbm, ci), (co_hbm, co), (bias_hbm, bias_row)]
        )
    ]
    for copy in given:
        copy.start()

    barrier = pltpu.get_barrier_semaphore()
    greet = [at(d, dx) for d in NEAR for dx in range(2)] + [at(0, 1)]
    greet += [(me_a, (me_b + d) & 15) for d in BA_STEPS]
    for peer in greet:
        pl.semaphore_signal(barrier, inc=1, device_id=peer, device_id_type=MESH)

    stage[0:16] = jnp.zeros((16, 256), F32)
    given[0].wait()
    for a in range(2):
        stage[a * 2 : a * 2 + 2] = fa[a].astype(F32)
    pa[...] = stage[0:16].astype(BF16)
    given[1].wait()
    for b in range(4):
        stage[16 + b * 4 : 20 + b * 4] = fb[b].astype(F32)
    pb[...] = stage[16:32].astype(BF16)
    pl.semaphore_wait(barrier, len(greet))
    for k, d in enumerate(NEAR):
        send(pb, gb.at[me_a], s_b.at[0], r_b.at[k], at(d))
    send(pb, gb.at[me_a], s_b.at[0], r_b.at[8], at(0, 1))
    for d in BA_STEPS:
        send(pa, ga.at[me_b], s_a.at[0], r_a.at[0], (me_a, (me_b + d) & 15))

    ga[pl.ds(me_b, 1)] = pa[...][None]
    gb[pl.ds(me_a, 1)] = pb[...][None]

    row = iota((128, 128), 0)
    perm_b = one_hot(((row >> 2) & 7) * 16 + (row >> 5) * 4 + (row & 3) == iota((128, 128), 1))
    row = iota((64, 256), 0)
    perm_a = one_hot(((row & 31) >> 1) * 16 + (row >> 5) * 2 + (row & 1) == iota((64, 256), 1))

    for d in reversed(NEAR):
        slot = at(d)[0]
        arrived(gb.at[slot], r_b.at[NEAR.index(-d)])
        targets = [at(0, 1)]
        if abs(d) == 4:
            away = [-4, -3, -2, -1] if d > 0 else [3, 2, 1]
            targets = [at(step, dx) for step in away for dx in (1, 0)] + targets
        for to in targets:
            send(gb.at[slot], gb.at[slot], s_b.at[0], r_b.at[8], to)
    arrived(ga.at[0:15], r_a.at[0])
    ax[64:128] = dot(perm_a, ga[...].reshape(256, 256)).astype(BF16)
    up_a, down_a = ((me_a + 1) & 31, me_b), ((me_a - 1) & 31, me_b)
    up_b, down_b = (me_a, (me_b + 1) & 15), (me_a, (me_b - 1) & 15)
    send(ax.at[64:128], ax.at[0:64], s_h.at[2], r_h.at[2], up_a)
    send(ax.at[64:128], ax.at[128:192], s_h.at[3], r_h.at[3], down_a)
    arrived(gb.at[0:23], r_b.at[8])
    for g in range(4):
        rows = dot(perm_b, gb[g * 8 : g * 8 + 8].reshape(128, 256)).astype(BF16)
        for b in range(4):
            bx[256 + b * 128 + g * 32 : 288 + b * 128 + g * 32] = rows[b * 32 : b * 32 + 32]

    send(bx.at[512:768], bx.at[0:256], s_h.at[0], r_h.at[0], up_b)
    send(bx.at[256:512], bx.at[768:1024], s_h.at[1], r_h.at[1], down_b)

    scores = dot_nt(ax[64:128], bx[256:768]) * (1.0 / 16.0)
    own[...] = scores
    lse_c, top_r, sum_r, _ = masses(scores)
    for b in range(4):
        na_src[b : b + 1] = lse_c[:, b * 128 : (b + 1) * 128]
    nb_src[...] = jnp.zeros((1, 128), F32)
    nb_src[:, 0:64] = to_row(top_r + jnp.log(sum_r))
    for dz, dx in AA_STEPS:
        send(na_src, na_all.at[me_a], s_na.at[0], r_na.at[0], at(dz, dx))
    for d in BA_STEPS:
        send(nb_src, nb_all.at[me_b], s_nb.at[0], r_nb.at[0], (me_a, (me_b + d) & 15))
    na_all[pl.ds(me_a, 1)] = na_src[...][None]
    nb_all[pl.ds(me_b, 1)] = nb_src[...][None]

    col = iota((8, 512), 1)
    d24 = div(col, 48)
    rest = col - 48 * d24
    a1, b1 = rest >> 3, rest & 7
    d2 = (d24 * 11) >> 5
    tap = (a1 * 9 + d2 * 3 + b1) * 8 + (d24 - 3 * d2)
    tap = jnp.where((a1 < 3) & (b1 < 3) & (col < 432), tap, -1)
    spread = one_hot(iota((256, 512), 0) == jnp.broadcast_to(tap[0:1], (256, 512)))
    taps_m[...] = jnp.zeros((512, 128), F32)
    for copy in given[2:]:
        copy.wait()
    for k in range(27):
        taps_m[k * 8 : k * 8 + 3, 0:8] = ci[k]
        taps_m[256 + k * 8 : 259 + k * 8, 0:8] = co[k]
    base = sum(
        lax.dot_general(part, spread, (((0,), (0,)), ((), ())), preferred_element_type=F32)
        for part in halves(taps_m[0:256])
    )[0:8]
    for p in range(24):
        s = (p // 6) * 8 + p % 6
        w1f[p * 8 : p * 8 + 8] = pltpu.roll(base, s, 1) if s else base
    for g in range(4):
        c = iota((8, 128), 1) + (g & 1) * 128
        d2 = (c * 820) >> 16
        c = c - 80 * d2
        d4 = (c * 2731) >> 16
        c = jnp.where((d4 < 3) & (d2 < 3), c - 24 * d4, -1000)
        b1 = (c & 3) + (2 if g < 2 else ((c & 2) << 1))
        target = (d2 * 3 + d4) * 48 + (c >> 2) * 8 + b1
        chosen = one_hot(iota((512, 128), 0) == jnp.broadcast_to(target[0:1], (512, 128)))
        for part, rows in zip(halves(w1f[...]), (slice(0, 192), slice(192, 384))):
            w1[rows, g * 128 : g * 128 + 128] = dot(part, chosen).astype(BF16)

    k, c = iota((256, 256), 0) >> 3, iota((256, 256), 1)
    k3 = (k * 11) >> 5
    k9 = div(k, 9)
    ca = div(c, 48)
    cb = (c - 48 * ca) >> 3
    pick = one_hot(iota((128, 256), 0) == (iota((128, 256), 1) & 7))
    high, low = halves(taps_m[256:512])
    taps = jnp.where((k9 == ca) & (k - 3 * k3 == cb), dot(high, pick) + dot(low, pick), 0.0)
    k = iota((16, 256), 1)
    k3, k9 = ((k >> 3) * 11) >> 5, div(k >> 3, 9)
    place = one_hot(iota((16, 256), 0) == (k3 - 3 * k9) * 3 + (k & 7))
    place = jnp.where((k & 7) < 3, place, jnp.zeros_like(place))
    base = select(place, taps)
    for o in range(8):
        s = (o // 4) * 48 + (o % 4) * 8
        w2f[o * 16 : o * 16 + 16] = pltpu.roll(base, s, 1) if s else base
    r, c = iota((72, 128), 0), iota((72, 128), 1)
    order = one_hot(c == (r & 7) * 16 + (r >> 3))
    c = iota((72, 256), 1)
    ca = div(c, 48)
    cb = (c - 48 * ca) >> 3
    ra, rb = 2 * me_a - 1 + ca, 4 * me_b - 1 + cb
    inside = (ra >= 0) & (ra < 64) & (rb >= 0) & (rb < 64)
    w2[0:72], w2[72:144] = halves(jnp.where(inside, select(order, w2f[...]), 0.0))
    bias = jnp.where(iota((8, 8), 0) == iota((8, 8), 1), bias_row[...], 0.0)
    bias = jnp.broadcast_to(jnp.sum(bias, axis=1, keepdims=True), (8, 128))
    bias = jnp.concatenate([jnp.concatenate([bias] * 24, axis=0)] * (WIDE // 128), axis=1)
    for x in (x3, x3_low):
        x[:, 0:128] = jnp.zeros((160, 128), BF16)
        x[:, 33 * 128 :] = jnp.zeros((160, 128), BF16)
    zs[:, 0:128] = jnp.zeros((72, 128), F32)
    zs[:, 33 * 128 :] = jnp.zeros((72, 128), F32)
    nb2_src[...] = jnp.zeros((1, 128), F32)
    ps[...] = jnp.zeros((256, 128), F32)

    arrived(bx.at[0:256], r_h.at[0])
    arrived(bx.at[768:1024], r_h.at[1])
    arrived(ax.at[0:64], r_h.at[2])
    arrived(ax.at[128:192], r_h.at[3])
    for t in range(3):
        sx[t * 64 : t * 64 + 64] = dot_nt(ax[t * 64 : t * 64 + 64], bx[...]) * (1.0 / 8.0)

    arrived(nb_all.at[0:15], r_nb.at[0])
    nb_own[...] = join(nb_all[...])
    send(nb_own, nb_lo, s_h.at[4], r_h.at[4], up_a)
    send(nb_own, nb_hi, s_h.at[5], r_h.at[5], down_a)
    arrived(na_all.at[0:31], r_na.at[0])
    na_own[...] = join(na_all[...])
    send(na_own, na_lo, s_h.at[6], r_h.at[6], up_b)
    send(na_own, na_hi, s_h.at[7], r_h.at[7], down_b)
    arrived(nb_lo, r_h.at[4])
    arrived(nb_hi, r_h.at[5])
    cols = [
        to_column(jnp.where(me_a > 0, nb_lo[...], FAR)),
        to_column(nb_own[...]),
        to_column(jnp.where(me_a < 31, nb_hi[...], FAR)),
    ]
    nar[2:6] = na_own[...] - OFFSET
    lane = iota((24, 128), 1)

    def match(side, columns):
        for t in range(3):
            for k, b in enumerate(columns):
                v = sx[t * 64 : t * 64 + 64, b * 128 : (b + 1) * 128] - cols[t] - nar[b : b + 1]
                v = jnp.maximum(v, 0.0) + jnp.log(1.0 + jnp.exp(-jnp.abs(v)))
                for a in range(2):
                    xt[pl.ds(side * 768 + t * 256 + a * 4 + k, 32, stride=8), :] = v[a * 32 : a * 32 + 32]
        for a2 in range(32):
            m = jnp.concatenate([xt[pl.ds(side * 768 + (t * 32 + a2) * 8, 8), :] for t in range(3)], axis=0)
            left = jnp.where(lane > 0, pltpu.roll(m, 1, 1), 0.0)
            right = jnp.where(lane < 127, pltpu.roll(m, 127, 1), 0.0)
            m = jnp.concatenate([left, m, right, jnp.zeros((8, 128), F32)], axis=0)
            rows, out = slice(side * 80, side * 80 + 80), slice((a2 + 1) * 128, (a2 + 2) * 128)
            x3[rows, out], x3_low[rows, out] = halves(m)

    def first(side, at2):
        rows, taps = slice(side * 80, side * 80 + 80), slice(side * 256, side * 256 + 240)
        high, low = (
            jnp.concatenate([x[rows, at2 + d * 128 : at2 + d * 128 + WIDE] for d in range(3)], axis=0)
            for x in (x3, x3_low)
        )
        out = dot(w1[:, taps], high)
        return out[0:192] + out[192:384] + dot(w1[0:192, taps], low)

    match(0, (2, 3, 4, 5))
    for g in range(4096 // WIDE):
        acc[:, g * WIDE : g * WIDE + WIDE] = first(0, g * WIDE) + bias
    arrived(na_lo, r_h.at[6])
    arrived(na_hi, r_h.at[7])
    nar[0:2] = jnp.where(me_b > 0, na_lo[2:4], FAR) - OFFSET
    nar[6:8] = jnp.where(me_b < 15, na_hi[0:2], FAR) - OFFSET
    match(1, (0, 1, 6, 7))
    side = iota((8, 128), 1)

    def second(a2):
        u = []
        for d4 in range(3):
            terms = [
                zs[(d * 3 + d4) * 8 : (d * 3 + d4) * 8 + 8, (a2 + d) * 128 : (a2 + d + 1) * 128]
                for d in range(3)
            ]
            u.append(terms[0] + terms[1] + terms[2])
        f = u[1] + jnp.where(side > 0, pltpu.roll(u[0], 1, 1), 0.0)
        f = f + jnp.where(side < 127, pltpu.roll(u[2], 127, 1), 0.0)
        ft[a2 * 8 : a2 * 8 + 8] = jnp.maximum(f, 0.0)

    for g in range(4096 // WIDE):
        at2 = g * WIDE
        hidden = acc[:, at2 : at2 + WIDE] + first(1, at2)
        high, low = halves(jnp.maximum(hidden, 0.0))
        out = dot(w2[:, 0:192], high)
        zs[:, at2 + 128 : at2 + 128 + WIDE] = out[0:72] + out[72:144] + dot(w2[0:72, 0:192], low)
        for a2 in range(max(at2 // 128 - 1, 0), (at2 + WIDE) // 128 - 1):
            second(a2)
    second(31)
    for a in range(2):
        for b in range(4):
            rows, lanes = slice(a * 32, a * 32 + 32), slice(b * 128, (b + 1) * 128)
            rn[rows, lanes] = own[rows, lanes] + ft[pl.ds(a * 4 + b, 32, stride=8), :]

    refined = rn[...]
    lse_c, top_r, sum_r, share = masses(refined)
    for b in range(4):
        na2_src[b : b + 1] = lse_c[:, b * 128 : (b + 1) * 128]
    for dz, dx in AA_STEPS:
        send(na2_src, na2_all.at[me_a], s_na2.at[0], r_na2.at[0], at(dz, dx))
    lse_r = top_r + jnp.log(sum_r)
    nb2_src[:, 0:64] = to_row(lse_r)
    for d in BA_STEPS:
        send(nb2_src, nb2_all.at[me_b], s_nb2.at[0], r_nb2.at[0], (me_a, (me_b + d) & 15))
    na2_all[pl.ds(me_a, 1)] = na2_src[...][None]
    nb2_all[pl.ds(me_b, 1)] = nb2_src[...][None]
    high, low = halves(share)
    features = bx[256:768]
    moved = (dot(high, features) + dot(low, features)) / sum_r
    pn[0:64] = moved[:, 0:128]
    pn[64:128] = moved[:, 128:256]
    pn[128:192] = jnp.broadcast_to(lse_r, (64, 128))
    for g in range(3):
        for q in range(4):
            rows = pl.ds(g * 64 + (q >> 1) * 32 + (q & 1), 16, stride=2)
            ps[pl.ds(g * 4 + q, 16, stride=16), :] = pn[rows, :]
    for d in BA_STEPS:
        to = (me_b + d) & 15
        block = ps.at[pl.ds(pl.multiple_of(to * 16, 16), 16)]
        send(block, pr.at[me_b], s_p.at[0], r_p.at[0], (me_a, to))
    pr[pl.ds(me_b, 1)] = ps[pl.ds(pl.multiple_of(me_b * 16, 16), 16), :][None]

    arrived(nb2_all.at[0:15], r_nb2.at[0])
    col = to_column(join(nb2_all[...])) - OFFSET
    arrived(pr.at[0:15], r_p.at[0])
    lse = pr[:, 8:12, :]
    weight = jnp.exp(lse - jnp.max(lse, axis=0, keepdims=True))
    total = jnp.sum(weight, axis=0)
    for g in range(2):
        moved = jnp.sum(weight * pr[:, g * 4 : g * 4 + 4, :], axis=0) / total
        for a in range(2):
            warped[a, :, g * 128 : g * 128 + 128] = moved[a * 2 : a * 2 + 2]
    twice = 2.0 * refined - col
    for ref, sem in [
        (gb.at[0:31], s_b.at[0]), (ga.at[0:15], s_a.at[0]), (na_all.at[0:31], s_na.at[0]), (nb_all.at[0:15], s_nb.at[0]),
        (na2_all.at[0:31], s_na2.at[0]), (nb2_all.at[0:15], s_nb2.at[0]), (pr.at[0:15], s_p.at[0]),
        (bx.at[0:256], s_h.at[0]), (bx.at[0:256], s_h.at[1]), (ax.at[0:64], s_h.at[2]), (ax.at[0:64], s_h.at[3]),
        (nb_own, s_h.at[4]), (nb_own, s_h.at[5]), (na_own, s_h.at[6]), (na_own, s_h.at[7]),
    ]:
        arrived(ref, sem)
    arrived(na2_all.at[0:31], r_na2.at[0])
    norm = join(na2_all[...])
    for b in range(4):
        lm[pl.ds(b, 64, stride=4), :] = twice[:, b * 128 : (b + 1) * 128] - norm[b : b + 1]


def place_results(lm, warped, lm_out, warped_out, s):
    copies = [pltpu.make_async_copy(lm, lm_out, s.at[0]), pltpu.make_async_copy(warped, warped_out, s.at[1])]
    for copy in copies:
        copy.start()
    for copy in copies:
        copy.wait()


def local(features_a, features_b, conv_in, bias_in, conv_out):
    ci = conv_in.transpose(1, 2, 3, 4, 0).reshape(27, 3, 8)
    co = conv_out.transpose(1, 2, 3, 4, 0).reshape(27, 3, 8)
    dma = pltpu.SemaphoreType.DMA
    vmem = pltpu.VMEM
    lm, warped = pl.pallas_call(
        kernel,
        out_shape=(jax.ShapeDtypeStruct((256, 128), F32), jax.ShapeDtypeStruct((2, 2, 256), F32)),
        in_specs=[pl.BlockSpec(memory_space=pltpu.HBM)] * 5,
        out_specs=(pl.BlockSpec(memory_space=pltpu.VMEM),) * 2,
        scratch_shapes=[
            vmem((2, 2, 256), BF16), vmem((4, 4, 256), BF16), vmem((27, 3, 8), F32), vmem((27, 3, 8), F32), vmem((1, 8), F32),
            vmem((32, 256), F32), vmem((512, 128), F32), vmem((16, 256), BF16), vmem((16, 256), BF16),
            vmem((16, 16, 256), BF16), vmem((32, 16, 256), BF16),
            vmem((192, 256), BF16), vmem((1024, 256), BF16),
            vmem((192, 512), F32), vmem((384, 512), BF16), vmem((128, 256), F32), vmem((144, 256), BF16),
            vmem((4, 128), F32), vmem((1, 128), F32), vmem((32, 4, 128), F32), vmem((16, 1, 128), F32),
            vmem((4, 128), F32), vmem((1, 128), F32), vmem((4, 128), F32), vmem((4, 128), F32),
            vmem((1, 128), F32), vmem((1, 128), F32),
            vmem((64, 512), F32), vmem((192, 1024), F32), vmem((1536, 128), F32),
            vmem((160, 34 * 128), BF16), vmem((160, 34 * 128), BF16), vmem((192, 4096), F32), vmem((72, 34 * 128), F32), vmem((256, 128), F32),
            vmem((64, 512), F32), vmem((192, 128), F32), vmem((256, 128), F32), vmem((16, 16, 128), F32),
            vmem((4, 128), F32), vmem((1, 128), F32), vmem((32, 4, 128), F32), vmem((16, 1, 128), F32),
            vmem((8, 128), F32),
            dma((1,)), dma((1,)), dma((1,)), dma((9,)), dma((8,)), dma((8,)),
            dma((1,)), dma((1,)), dma((1,)), dma((1,)),
            dma((1,)), dma((1,)), dma((1,)), dma((1,)), dma((1,)), dma((1,)), dma((5,)),
        ],
        compiler_params=pltpu.CompilerParams(
            collective_id=0, has_side_effects=True, vmem_limit_bytes=60 * 2**20
        ),
        cost_estimate=pl.CostEstimate(flops=2 * 10**9, bytes_accessed=10**6, transcendentals=10**6),
    )(features_a, features_b, ci, co, bias_in.reshape(1, 8))
    lm = lm.reshape(2, 32, 4, 128)
    return pl.pallas_call(
        place_results,
        out_shape=(jax.ShapeDtypeStruct(lm.shape, F32), jax.ShapeDtypeStruct(warped.shape, F32)),
        in_specs=[pl.BlockSpec(memory_space=pltpu.VMEM)] * 2,
        out_specs=(pl.BlockSpec(memory_space=pltpu.HBM),) * 2,
        scratch_shapes=[dma((2,))],
        compiler_params=pltpu.CompilerParams(vmem_limit_bytes=60 * 2**20),
    )(lm, warped)


def solution(mesh):
    placed = (P("aa", "ba", None), P("ba", "aa", None), P(), P(), P())
    return jax.shard_map(
        local,
        mesh=mesh,
        in_specs=placed,
        out_specs=(P("aa", None, "ba", None), P("aa", "ba", None)),
        check_vma=False,
    )
```

```python
import math

import jax
import jax.numpy as jnp
from jax import lax
from jax.experimental import pallas as pl
from jax.experimental.pallas import tpu as pltpu
from jax.sharding import PartitionSpec as P

F32, BF16, I32 = jnp.float32, jnp.bfloat16, jnp.int32
MESH = pl.DeviceIdType.MESH
OFFSET = math.log(64 * 32 * 64 * 128)
FAR = 1e30
WIDE = 2048

AA_STEPS = sorted(
    [(dz, dx) for dz in range(-7, 9) for dx in range(2) if dz or dx],
    key=lambda o: -(abs(o[0]) + 2 * o[1]),
)
BA_STEPS = [15, 14, 13, 12, 11, 10, 9, 8, 7, 6, 5, 4, 3, 2, 1]
NEAR = [4, -4, 3, -3, 2, -2, 1, -1]


def iota(shape, dim):
    return lax.broadcasted_iota(I32, shape, dim)


def div(x, by):
    return (x * {3: 21846, 9: 7282, 27: 2428, 48: 1366}[by]) >> 16


def one_hot(mask):
    return jnp.where(mask, 1.0, 0.0).astype(BF16)


def dot(a, b):
    return jnp.dot(a, b, preferred_element_type=F32)


def dot_nt(a, b):
    return lax.dot_general(a, b, (((1,), (1,)), ((), ())), preferred_element_type=F32)


def halves(x):
    high = x.astype(BF16)
    return high, (x - high.astype(F32)).astype(BF16)


def select(chosen, x):
    high, low = halves(x)
    return dot(chosen, high) + dot(chosen, low)


def to_row(column):
    wide = jnp.broadcast_to(column, (64, 128))
    return jnp.concatenate([wide, wide], axis=0).T[0:1, 0:64]


def to_column(row):
    return jnp.broadcast_to(row, (128, 128)).T[0:64, 0:1]


def masses(cells):
    top_c = jnp.max(cells, axis=0, keepdims=True)
    lse_c = top_c + jnp.log(jnp.sum(jnp.exp(cells - top_c), axis=0, keepdims=True))
    top_r = jnp.max(cells, axis=1, keepdims=True)
    share = jnp.exp(cells - top_r)
    sum_r = jnp.sum(share, axis=1, keepdims=True)
    return lse_c, top_r, sum_r, share


def join(parts):
    top = jnp.max(parts, axis=0)
    return top + jnp.log(jnp.sum(jnp.exp(parts - top[None]), axis=0))


def kernel(
    fa_hbm, fb_hbm, ci_hbm, co_hbm, bias_hbm, lm, warped,
    fa, fb, ci, co, bias_row, stage, taps_m, pa, pb, ga, gb, ax, bx, w1f, w1, w2f, w2,
    na_src, nb_src, na_all, nb_all, na_own, nb_own, na_lo, na_hi, nb_lo, nb_hi,
    own, sx, xt, x3, x3_low, acc, zs, ft, rn, pn, ps, pr,
    na2_src, nb2_src, na2_all, nb2_all, nar,
    s_a, r_a, s_b, r_b, s_h, r_h, s_na, r_na, s_nb, r_nb, s_na2, r_na2, s_nb2, r_nb2, s_p, r_p, s_in,
):
    me_a, me_b = lax.axis_index("aa"), lax.axis_index("ba")
    z, xh = me_a >> 1, me_a & 1

    def at(dz, dx=0):
        return ((((z + dz) & 15) << 1) | ((xh + dx) & 1), me_b)

    def send(src, dst, s, r, to):
        copy = pltpu.make_async_remote_copy(
            src_ref=src, dst_ref=dst, send_sem=s, recv_sem=r, device_id=to, device_id_type=MESH
        )
        copy.start()

    def arrived(ref, r):
        pltpu.make_async_remote_copy(
            src_ref=ref, dst_ref=ref, send_sem=r, recv_sem=r, device_id=at(0, 1), device_id_type=MESH
        ).wait_recv()

    given = [
        pltpu.make_async_copy(src, dst, s_in.at[k])
        for k, (src, dst) in enumerate(
            [(fa_hbm, fa), (fb_hbm, fb), (ci_hbm, ci), (co_hbm, co), (bias_hbm, bias_row)]
        )
    ]
    for copy in given:
        copy.start()

    barrier = pltpu.get_barrier_semaphore()
    greet = [at(d, dx) for d in NEAR for dx in range(2)] + [at(0, 1)]
    greet += [(me_a, (me_b + d) & 15) for d in BA_STEPS]
    for peer in greet:
        pl.semaphore_signal(barrier, inc=1, device_id=peer, device_id_type=MESH)

    stage[0:16] = jnp.zeros((16, 256), F32)
    given[0].wait()
    for a in range(2):
        stage[a * 2 : a * 2 + 2] = fa[a].astype(F32)
    pa[...] = stage[0:16].astype(BF16)
    given[1].wait()
    for b in range(4):
        stage[16 + b * 4 : 20 + b * 4] = fb[b].astype(F32)
    pb[...] = stage[16:32].astype(BF16)
    pl.semaphore_wait(barrier, len(greet))
    for k, d in enumerate(NEAR):
        send(pb, gb.at[me_a], s_b.at[0], r_b.at[k], at(d))
    send(pb, gb.at[me_a], s_b.at[0], r_b.at[8], at(0, 1))
    for d in BA_STEPS:
        send(pa, ga.at[me_b], s_a.at[0], r_a.at[0], (me_a, (me_b + d) & 15))

    ga[pl.ds(me_b, 1)] = pa[...][None]
    gb[pl.ds(me_a, 1)] = pb[...][None]

    row = iota((128, 128), 0)
    perm_b = one_hot(((row >> 2) & 7) * 16 + (row >> 5) * 4 + (row & 3) == iota((128, 128), 1))
    row = iota((64, 256), 0)
    perm_a = one_hot(((row & 31) >> 1) * 16 + (row >> 5) * 2 + (row & 1) == iota((64, 256), 1))

    for d in reversed(NEAR):
        slot = at(d)[0]
        arrived(gb.at[slot], r_b.at[NEAR.index(-d)])
        targets = [at(0, 1)]
        if abs(d) == 4:
            away = [-4, -3, -2, -1] if d > 0 else [3, 2, 1]
            targets = [at(step, dx) for step in away for dx in (1, 0)] + targets
        for to in targets:
            send(gb.at[slot], gb.at[slot], s_b.at[0], r_b.at[8], to)
    arrived(ga.at[0:15], r_a.at[0])
    ax[64:128] = dot(perm_a, ga[...].reshape(256, 256)).astype(BF16)
    up_a, down_a = ((me_a + 1) & 31, me_b), ((me_a - 1) & 31, me_b)
    up_b, down_b = (me_a, (me_b + 1) & 15), (me_a, (me_b - 1) & 15)
    send(ax.at[64:128], ax.at[0:64], s_h.at[2], r_h.at[2], up_a)
    send(ax.at[64:128], ax.at[128:192], s_h.at[3], r_h.at[3], down_a)
    arrived(gb.at[0:23], r_b.at[8])
    for g in range(4):
        rows = dot(perm_b, gb[g * 8 : g * 8 + 8].reshape(128, 256)).astype(BF16)
        for b in range(4):
            bx[256 + b * 128 + g * 32 : 288 + b * 128 + g * 32] = rows[b * 32 : b * 32 + 32]

    send(bx.at[512:768], bx.at[0:256], s_h.at[0], r_h.at[0], up_b)
    send(bx.at[256:512], bx.at[768:1024], s_h.at[1], r_h.at[1], down_b)

    scores = dot_nt(ax[64:128], bx[256:768]) * (1.0 / 16.0)
    own[...] = scores
    lse_c, top_r, sum_r, _ = masses(scores)
    for b in range(4):
        na_src[b : b + 1] = lse_c[:, b * 128 : (b + 1) * 128]
    nb_src[...] = jnp.zeros((1, 128), F32)
    nb_src[:, 0:64] = to_row(top_r + jnp.log(sum_r))
    for dz, dx in AA_STEPS:
        send(na_src, na_all.at[me_a], s_na.at[0], r_na.at[0], at(dz, dx))
    for d in BA_STEPS:
        send(nb_src, nb_all.at[me_b], s_nb.at[0], r_nb.at[0], (me_a, (me_b + d) & 15))
    na_all[pl.ds(me_a, 1)] = na_src[...][None]
    nb_all[pl.ds(me_b, 1)] = nb_src[...][None]

    col = iota((8, 512), 1)
    d24 = div(col, 48)
    rest = col - 48 * d24
    a1, b1 = rest >> 3, rest & 7
    d2 = (d24 * 11) >> 5
    tap = (a1 * 9 + d2 * 3 + b1) * 8 + (d24 - 3 * d2)
    tap = jnp.where((a1 < 3) & (b1 < 3) & (col < 432), tap, -1)
    spread = one_hot(iota((256, 512), 0) == jnp.broadcast_to(tap[0:1], (256, 512)))
    taps_m[...] = jnp.zeros((512, 128), F32)
    for copy in given[2:]:
        copy.wait()
    for k in range(27):
        taps_m[k * 8 : k * 8 + 3, 0:8] = ci[k]
        taps_m[256 + k * 8 : 259 + k * 8, 0:8] = co[k]
    base = sum(
        lax.dot_general(part, spread, (((0,), (0,)), ((), ())), preferred_element_type=F32)
        for part in halves(taps_m[0:256])
    )[0:8]
    for p in range(24):
        s = (p // 6) * 8 + p % 6
        w1f[p * 8 : p * 8 + 8] = pltpu.roll(base, s, 1) if s else base
    for g in range(4):
        c = iota((8, 128), 1) + (g & 1) * 128
        d2 = (c * 820) >> 16
        c = c - 80 * d2
        d4 = (c * 2731) >> 16
        c = jnp.where((d4 < 3) & (d2 < 3), c - 24 * d4, -1000)
        b1 = (c & 3) + (2 if g < 2 else ((c & 2) << 1))
        target = (d2 * 3 + d4) * 48 + (c >> 2) * 8 + b1
        chosen = one_hot(iota((512, 128), 0) == jnp.broadcast_to(target[0:1], (512, 128)))
        for part, rows in zip(halves(w1f[...]), (slice(0, 192), slice(192, 384))):
            w1[rows, g * 128 : g * 128 + 128] = dot(part, chosen).astype(BF16)

    k, c = iota((256, 256), 0) >> 3, iota((256, 256), 1)
    k3 = (k * 11) >> 5
    k9 = div(k, 9)
    ca = div(c, 48)
    cb = (c - 48 * ca) >> 3
    pick = one_hot(iota((128, 256), 0) == (iota((128, 256), 1) & 7))
    high, low = halves(taps_m[256:512])
    taps = jnp.where((k9 == ca) & (k - 3 * k3 == cb), dot(high, pick) + dot(low, pick), 0.0)
    k = iota((16, 256), 1)
    k3, k9 = ((k >> 3) * 11) >> 5, div(k >> 3, 9)
    place = one_hot(iota((16, 256), 0) == (k3 - 3 * k9) * 3 + (k & 7))
    place = jnp.where((k & 7) < 3, place, jnp.zeros_like(place))
    base = select(place, taps)
    for o in range(8):
        s = (o // 4) * 48 + (o % 4) * 8
        w2f[o * 16 : o * 16 + 16] = pltpu.roll(base, s, 1) if s else base
    r, c = iota((72, 128), 0), iota((72, 128), 1)
    order = one_hot(c == (r & 7) * 16 + (r >> 3))
    c = iota((72, 256), 1)
    ca = div(c, 48)
    cb = (c - 48 * ca) >> 3
    ra, rb = 2 * me_a - 1 + ca, 4 * me_b - 1 + cb
    inside = (ra >= 0) & (ra < 64) & (rb >= 0) & (rb < 64)
    w2[0:72], w2[72:144] = halves(jnp.where(inside, select(order, w2f[...]), 0.0))
    bias = jnp.where(iota((8, 8), 0) == iota((8, 8), 1), bias_row[...], 0.0)
    bias = jnp.broadcast_to(jnp.sum(bias, axis=1, keepdims=True), (8, 128))
    bias = jnp.concatenate([jnp.concatenate([bias] * 24, axis=0)] * (WIDE // 128), axis=1)
    for x in (x3, x3_low):
        x[:, 0:128] = jnp.zeros((160, 128), BF16)
        x[:, 33 * 128 :] = jnp.zeros((160, 128), BF16)
    zs[:, 0:128] = jnp.zeros((72, 128), F32)
    zs[:, 33 * 128 :] = jnp.zeros((72, 128), F32)
    nb2_src[...] = jnp.zeros((1, 128), F32)
    ps[...] = jnp.zeros((256, 128), F32)

    arrived(bx.at[0:256], r_h.at[0])
    arrived(bx.at[768:1024], r_h.at[1])
    arrived(ax.at[0:64], r_h.at[2])
    arrived(ax.at[128:192], r_h.at[3])
    for t in range(3):
        sx[t * 64 : t * 64 + 64] = dot_nt(ax[t * 64 : t * 64 + 64], bx[...]) * (1.0 / 8.0)

    arrived(nb_all.at[0:15], r_nb.at[0])
    nb_own[...] = join(nb_all[...])
    send(nb_own, nb_lo, s_h.at[4], r_h.at[4], up_a)
    send(nb_own, nb_hi, s_h.at[5], r_h.at[5], down_a)
    arrived(na_all.at[0:31], r_na.at[0])
    na_own[...] = join(na_all[...])
    send(na_own, na_lo, s_h.at[6], r_h.at[6], up_b)
    send(na_own, na_hi, s_h.at[7], r_h.at[7], down_b)
    arrived(nb_lo, r_h.at[4])
    arrived(nb_hi, r_h.at[5])
    cols = [
        to_column(jnp.where(me_a > 0, nb_lo[...], FAR)),
        to_column(nb_own[...]),
        to_column(jnp.where(me_a < 31, nb_hi[...], FAR)),
    ]
    nar[2:6] = na_own[...] - OFFSET
    lane = iota((24, 128), 1)

    def match(side, columns):
        for t in range(3):
            for k, b in enumerate(columns):
                v = sx[t * 64 : t * 64 + 64, b * 128 : (b + 1) * 128] - cols[t] - nar[b : b + 1]
                v = jnp.maximum(v, 0.0) + jnp.log(1.0 + jnp.exp(-jnp.abs(v)))
                for a in range(2):
                    xt[pl.ds(side * 768 + t * 256 + a * 4 + k, 32, stride=8), :] = v[a * 32 : a * 32 + 32]
        for a2 in range(32):
            m = jnp.concatenate([xt[pl.ds(side * 768 + (t * 32 + a2) * 8, 8), :] for t in range(3)], axis=0)
            left = jnp.where(lane > 0, pltpu.roll(m, 1, 1), 0.0)
            right = jnp.where(lane < 127, pltpu.roll(m, 127, 1), 0.0)
            m = jnp.concatenate([left, m, right, jnp.zeros((8, 128), F32)], axis=0)
            rows, out = slice(side * 80, side * 80 + 80), slice((a2 + 1) * 128, (a2 + 2) * 128)
            x3[rows, out], x3_low[rows, out] = halves(m)

    def first(side, at2):
        rows, taps = slice(side * 80, side * 80 + 80), slice(side * 256, side * 256 + 240)
        high, low = (
            jnp.concatenate([x[rows, at2 + d * 128 : at2 + d * 128 + WIDE] for d in range(3)], axis=0)
            for x in (x3, x3_low)
        )
        tall = jnp.concatenate([high, high, low], axis=0)
        wide = jnp.concatenate([w1[0:192, taps], w1[192:384, taps], w1[0:192, taps]], axis=1)
        return dot(wide, tall)

    match(0, (2, 3, 4, 5))
    for g in range(4096 // WIDE):
        acc[:, g * WIDE : g * WIDE + WIDE] = first(0, g * WIDE) + bias
    arrived(na_lo, r_h.at[6])
    arrived(na_hi, r_h.at[7])
    nar[0:2] = jnp.where(me_b > 0, na_lo[2:4], FAR) - OFFSET
    nar[6:8] = jnp.where(me_b < 15, na_hi[0:2], FAR) - OFFSET
    match(1, (0, 1, 6, 7))
    side = iota((8, 128), 1)

    def second(a2):
        u = []
        for d4 in range(3):
            terms = [
                zs[(d * 3 + d4) * 8 : (d * 3 + d4) * 8 + 8, (a2 + d) * 128 : (a2 + d + 1) * 128]
                for d in range(3)
            ]
            u.append(terms[0] + terms[1] + terms[2])
        f = u[1] + jnp.where(side > 0, pltpu.roll(u[0], 1, 1), 0.0)
        f = f + jnp.where(side < 127, pltpu.roll(u[2], 127, 1), 0.0)
        ft[a2 * 8 : a2 * 8 + 8] = jnp.maximum(f, 0.0)

    for g in range(4096 // WIDE):
        at2 = g * WIDE
        hidden = acc[:, at2 : at2 + WIDE] + first(1, at2)
        high, low = halves(jnp.maximum(hidden, 0.0))
        out = dot(w2[:, 0:192], high)
        zs[:, at2 + 128 : at2 + 128 + WIDE] = out[0:72] + out[72:144] + dot(w2[0:72, 0:192], low)
        for a2 in range(max(at2 // 128 - 1, 0), (at2 + WIDE) // 128 - 1):
            second(a2)
    second(31)
    for a in range(2):
        for b in range(4):
            rows, lanes = slice(a * 32, a * 32 + 32), slice(b * 128, (b + 1) * 128)
            rn[rows, lanes] = own[rows, lanes] + ft[pl.ds(a * 4 + b, 32, stride=8), :]

    refined = rn[...]
    lse_c, top_r, sum_r, share = masses(refined)
    for b in range(4):
        na2_src[b : b + 1] = lse_c[:, b * 128 : (b + 1) * 128]
    for dz, dx in AA_STEPS:
        send(na2_src, na2_all.at[me_a], s_na2.at[0], r_na2.at[0], at(dz, dx))
    lse_r = top_r + jnp.log(sum_r)
    nb2_src[:, 0:64] = to_row(lse_r)
    for d in BA_STEPS:
        send(nb2_src, nb2_all.at[me_b], s_nb2.at[0], r_nb2.at[0], (me_a, (me_b + d) & 15))
    na2_all[pl.ds(me_a, 1)] = na2_src[...][None]
    nb2_all[pl.ds(me_b, 1)] = nb2_src[...][None]
    high, low = halves(share)
    features = bx[256:768]
    moved = (dot(high, features) + dot(low, features)) / sum_r
    pn[0:64] = moved[:, 0:128]
    pn[64:128] = moved[:, 128:256]
    pn[128:192] = jnp.broadcast_to(lse_r, (64, 128))
    for g in range(3):
        for q in range(4):
            rows = pl.ds(g * 64 + (q >> 1) * 32 + (q & 1), 16, stride=2)
            ps[pl.ds(g * 4 + q, 16, stride=16), :] = pn[rows, :]
    for d in BA_STEPS:
        to = (me_b + d) & 15
        block = ps.at[pl.ds(pl.multiple_of(to * 16, 16), 16)]
        send(block, pr.at[me_b], s_p.at[0], r_p.at[0], (me_a, to))
    pr[pl.ds(me_b, 1)] = ps[pl.ds(pl.multiple_of(me_b * 16, 16), 16), :][None]

    arrived(nb2_all.at[0:15], r_nb2.at[0])
    col = to_column(join(nb2_all[...])) - OFFSET
    arrived(pr.at[0:15], r_p.at[0])
    lse = pr[:, 8:12, :]
    weight = jnp.exp(lse - jnp.max(lse, axis=0, keepdims=True))
    total = jnp.sum(weight, axis=0)
    for g in range(2):
        moved = jnp.sum(weight * pr[:, g * 4 : g * 4 + 4, :], axis=0) / total
        for a in range(2):
            warped[a, :, g * 128 : g * 128 + 128] = moved[a * 2 : a * 2 + 2]
    twice = 2.0 * refined - col
    for ref, sem in [
        (gb.at[0:31], s_b.at[0]), (ga.at[0:15], s_a.at[0]), (na_all.at[0:31], s_na.at[0]), (nb_all.at[0:15], s_nb.at[0]),
        (na2_all.at[0:31], s_na2.at[0]), (nb2_all.at[0:15], s_nb2.at[0]), (pr.at[0:15], s_p.at[0]),
        (bx.at[0:256], s_h.at[0]), (bx.at[0:256], s_h.at[1]), (ax.at[0:64], s_h.at[2]), (ax.at[0:64], s_h.at[3]),
        (nb_own, s_h.at[4]), (nb_own, s_h.at[5]), (na_own, s_h.at[6]), (na_own, s_h.at[7]),
    ]:
        arrived(ref, sem)
    arrived(na2_all.at[0:31], r_na2.at[0])
    norm = join(na2_all[...])
    for b in range(4):
        lm[pl.ds(b, 64, stride=4), :] = twice[:, b * 128 : (b + 1) * 128] - norm[b : b + 1]


def place_results(lm, warped, lm_out, warped_out, s):
    copies = [pltpu.make_async_copy(lm, lm_out, s.at[0]), pltpu.make_async_copy(warped, warped_out, s.at[1])]
    for copy in copies:
        copy.start()
    for copy in copies:
        copy.wait()


def local(features_a, features_b, conv_in, bias_in, conv_out):
    ci = conv_in.transpose(1, 2, 3, 4, 0).reshape(27, 3, 8)
    co = conv_out.transpose(1, 2, 3, 4, 0).reshape(27, 3, 8)
    dma = pltpu.SemaphoreType.DMA
    vmem = pltpu.VMEM
    lm, warped = pl.pallas_call(
        kernel,
        out_shape=(jax.ShapeDtypeStruct((256, 128), F32), jax.ShapeDtypeStruct((2, 2, 256), F32)),
        in_specs=[pl.BlockSpec(memory_space=pltpu.HBM)] * 5,
        out_specs=(pl.BlockSpec(memory_space=pltpu.VMEM),) * 2,
        scratch_shapes=[
            vmem((2, 2, 256), BF16), vmem((4, 4, 256), BF16), vmem((27, 3, 8), F32), vmem((27, 3, 8), F32), vmem((1, 8), F32),
            vmem((32, 256), F32), vmem((512, 128), F32), vmem((16, 256), BF16), vmem((16, 256), BF16),
            vmem((16, 16, 256), BF16), vmem((32, 16, 256), BF16),
            vmem((192, 256), BF16), vmem((1024, 256), BF16),
            vmem((192, 512), F32), vmem((384, 512), BF16), vmem((128, 256), F32), vmem((144, 256), BF16),
            vmem((4, 128), F32), vmem((1, 128), F32), vmem((32, 4, 128), F32), vmem((16, 1, 128), F32),
            vmem((4, 128), F32), vmem((1, 128), F32), vmem((4, 128), F32), vmem((4, 128), F32),
            vmem((1, 128), F32), vmem((1, 128), F32),
            vmem((64, 512), F32), vmem((192, 1024), F32), vmem((1536, 128), F32),
            vmem((160, 34 * 128), BF16), vmem((160, 34 * 128), BF16), vmem((192, 4096), F32), vmem((72, 34 * 128), F32), vmem((256, 128), F32),
            vmem((64, 512), F32), vmem((192, 128), F32), vmem((256, 128), F32), vmem((16, 16, 128), F32),
            vmem((4, 128), F32), vmem((1, 128), F32), vmem((32, 4, 128), F32), vmem((16, 1, 128), F32),
            vmem((8, 128), F32),
            dma((1,)), dma((1,)), dma((1,)), dma((9,)), dma((8,)), dma((8,)),
            dma((1,)), dma((1,)), dma((1,)), dma((1,)),
            dma((1,)), dma((1,)), dma((1,)), dma((1,)), dma((1,)), dma((1,)), dma((5,)),
        ],
        compiler_params=pltpu.CompilerParams(
            collective_id=0, has_side_effects=True, vmem_limit_bytes=60 * 2**20
        ),
        cost_estimate=pl.CostEstimate(flops=2 * 10**9, bytes_accessed=10**6, transcendentals=10**6),
    )(features_a, features_b, ci, co, bias_in.reshape(1, 8))
    lm = lm.reshape(2, 32, 4, 128)
    return pl.pallas_call(
        place_results,
        out_shape=(jax.ShapeDtypeStruct(lm.shape, F32), jax.ShapeDtypeStruct(warped.shape, F32)),
        in_specs=[pl.BlockSpec(memory_space=pltpu.VMEM)] * 2,
        out_specs=(pl.BlockSpec(memory_space=pltpu.HBM),) * 2,
        scratch_shapes=[dma((2,))],
        compiler_params=pltpu.CompilerParams(vmem_limit_bytes=60 * 2**20),
    )(lm, warped)


def solution(mesh):
    placed = (P("aa", "ba", None), P("ba", "aa", None), P(), P(), P())
    return jax.shard_map(
        local,
        mesh=mesh,
        in_specs=placed,
        out_specs=(P("aa", None, "ba", None), P("aa", "ba", None)),
        check_vma=False,
    )
```
